32 devices in a mesh: blk: 16 (over z, y, x), rep: 2 (over core).
Axes of the slice: x: 2, y: 2, z: 4, core: 2. Of those that a mesh axis runs over, the one named last changes fastest.
Arguments:
- sky_map: float32 [512, 32768], P('blk', 'rep'), may hold values from -6 to 6
- noise_weight: float32 [512, 32768], P('blk', 'rep'), may hold values from 0.25 to 4
- prior_weight: float32 [128, 4, 2, 128], P('blk', 'rep'), may hold values from 0.5 to 4
- seeds: float32 [128, 4, 2, 512], P('blk', 'rep'), may hold values from -5 to 5
- loop_cos: float32 [512], replicated, may hold values from -0.3 to 0.3
- pair_m: int32 [128, 2], replicated, may hold values from 1 to 14939
- block_count: int32 [128], P('blk'), may hold values from 1 to 3, as said below
Outputs:
- solution: float32 [128, 4, 2, 128], P('blk', 'rep')
- residual: float32 [128, 4, 2, 128], P('blk', 'rep')
The draws below stay inside these ranges and needn't reach their ends.
Inputs may be any that keep to these rules, and one draw needn't show every extreme that they name: `pair_m`: each pair holds two m-columns; values may repeat between pairs. Pair p's first block_count[p] l-blocks belong to its first column, the other 4 - block_count[p] to its second.
All inputs are finite; a program needn't handle non-finite values.
Results may differ from the reference program's by a relative error of at most 0.00045.
Values sent between devices are 32-bit elements; how exact they have to be, the bound alone decides.
A program may use at most 128 MiB of HBM per device.

```python
import math
import jax
import jax.numpy as jnp
from jax import lax

NPHI = 32768
NBP = 4
ITERS = 2
NRING = 512
NPAIRS = 128
NCOL = 256
MMAX = 14939


def draw_block_count(key, part):
    counts = 1 + jnp.arange(NPAIRS, dtype=jnp.int32) % (NBP - 1)
    return jax.random.permutation(key, counts).astype(jnp.int32)


def set_ends(values, own_key, low, high):
    place = [jax.random.randint(jax.random.fold_in(own_key, axis), (), 0, length) for axis, length in enumerate(values.shape)]
    longest = values.shape.index(max(values.shape))
    next_to = place[:longest] + [(place[longest] + 1) % values.shape[longest]] + place[longest + 1:]
    return values.at[tuple(place)].set(low).at[tuple(next_to)].set(high)


def levels(own_key, extent, shards, low, high):
    level, own = 1.0, jax.random.fold_in(own_key, 6)
    for dim, parts in shards:
        draws = jnp.exp(jax.random.uniform(jax.random.fold_in(own, dim), (parts,), jnp.float32, low / len(shards), high / len(shards)))
        level = level * jnp.repeat(draws, extent[dim] // parts).reshape([-1 if axis == dim else 1 for axis in range(len(extent))])
    return level


def noise(rng, dims, scale, limit, split=(), held_as=jnp.bfloat16):
    entries = scale * jax.random.normal(rng, dims, jnp.float32)
    if split:
        entries = entries * levels(rng, dims, split, -0.22, 0.18)
    return jnp.clip(entries, -limit, limit).astype(held_as)


def setup_inputs(seed: int = 0) -> dict:
    key_list = jax.random.split(jax.random.key(seed), 8)
    sky_map = noise(key_list[0], (NRING, NPHI), 1.0, 6.0, ((0, 16), (1, 2)), jnp.float32)
    noise_weight = jnp.clip(jnp.exp(math.log(4.0) - 2.7725887 * jax.random.uniform(key_list[1], (NRING, NPHI), jnp.float32) ** levels(key_list[1], (NRING, NPHI), ((0, 16), (1, 2)), -0.2, 0.2)), 0.25, 4.0)
    prior_weight = jnp.clip(jnp.exp(math.log(4.0) - 2.0794415 * jax.random.uniform(key_list[2], (NPAIRS, NBP, 2, 128), jnp.float32) ** levels(key_list[2], (NPAIRS, NBP, 2, 128), ((0, 16), (1, 2)), -0.2, 0.2)), 0.5, 4.0)
    seeds = noise(key_list[3], (NPAIRS, NBP, 2, NRING), 1.0, 5.0, ((0, 16), (1, 2)), jnp.float32)
    loop_cos = jnp.clip(jax.random.uniform(key_list[4], (NRING,), jnp.float32, -0.3, 0.3), -0.3, 0.3)
    pair_m = set_ends(jax.random.randint(key_list[5], (NPAIRS, 2), 1, MMAX + 1), jax.random.fold_in(key_list[5], 1), 1, MMAX).astype(jnp.int32)
    block_count = draw_block_count(jax.random.fold_in(key_list[7], 71), 0)
    return dict(sky_map=sky_map, noise_weight=noise_weight, prior_weight=prior_weight, seeds=seeds, loop_cos=loop_cos, pair_m=pair_m, block_count=block_count)


EXACT = lax.Precision.HIGHEST

def block_layout(pair_m, block_count, block_ids):
    block_side = (block_ids[None, :] >= block_count[:, None]).astype(jnp.int32)
    offset = jnp.where(block_side == 0, block_ids[None, :], block_ids[None, :] - block_count[:, None])
    column_m = jnp.where(block_side == 0, pair_m[:, 0:1], pair_m[:, 1:2])
    block_start = 128 * (17 * column_m // 2048 + 1) + 128 * offset
    return (block_side, column_m, block_start)

def ladder(degree, column_m):
    degree_f = degree.astype(jnp.float32)
    m_over_l = column_m.astype(jnp.float32) / degree_f
    return jnp.sqrt((4.0 - 1.0 / (degree_f * degree_f)) / ((1.0 - m_over_l) * (1.0 + m_over_l)))

def legendre_rows(column_m, block_start, seeds, loop_cos, visit, initial):
    carried, first_out = visit(initial, seeds[:, 0], 0)
    carried, second_out = visit(carried, seeds[:, 1], 1)

    def advance(packed, step_id):
        earlier, latest, totals = packed
        degree = block_start + step_id
        coef_now = ladder(degree, column_m)[:, None]
        coef_prev = ladder(degree - 1, column_m)[:, None]
        current = coef_now * (loop_cos[None, :] * latest - earlier / coef_prev)
        totals, emitted = visit(totals, current, step_id)
        return ((latest, current, totals), emitted)
    (_, _, carried), others = lax.scan(advance, (seeds[:, 0], seeds[:, 1], carried), jnp.arange(2, 128, dtype=jnp.int32), unroll=8)
    return (carried, first_out, second_out, others)

def sum_columns(coef, block_side, column_m, block_start, seeds, loop_cos):
    pair_total, block_total = block_side.shape
    count_all = pair_total * block_total
    loop_total = loop_cos.shape[0]
    flat_coef = coef.reshape(count_all, 2, 128)

    def visit(totals, current, step_id):
        weight = lax.dynamic_index_in_dim(flat_coef, step_id, 2, keepdims=False)
        return (totals + weight[:, :, None] * current[:, None, :], None)
    totals, _, _, _ = legendre_rows(column_m.reshape(count_all), block_start.reshape(count_all), seeds.reshape(count_all, 2, loop_total), loop_cos, visit, jnp.zeros((count_all, 2, loop_total), jnp.float32))
    member = (block_side[:, :, None] == jnp.arange(2, dtype=jnp.int32)[None, None, :]).astype(jnp.float32)
    summed = jnp.einsum('pbs,pbtr->tpsr', member, totals.reshape(pair_total, block_total, 2, loop_total), precision=EXACT)
    return summed.reshape(2, 2 * pair_total, loop_total)

def spread_columns(spectra, block_side, column_m, block_start, seeds, loop_cos):
    pair_total, block_total = block_side.shape
    count_all = pair_total * block_total
    loop_total = loop_cos.shape[0]
    by_side = spectra.reshape(2, pair_total, 2, loop_total)
    side_zero = jnp.transpose(by_side[:, :, 0], (1, 0, 2))[:, None]
    side_one = jnp.transpose(by_side[:, :, 1], (1, 0, 2))[:, None]
    chosen = jnp.where(block_side[:, :, None, None] == 0, side_zero, side_one)
    flat_spec = chosen.reshape(count_all, 2, loop_total)

    def visit(carried, current, step_id):
        return (carried, lax.optimization_barrier(jnp.sum(current[:, None, :] * flat_spec, axis=2)))
    _, first_out, second_out, others = legendre_rows(column_m.reshape(count_all), block_start.reshape(count_all), seeds.reshape(count_all, 2, loop_total), loop_cos, visit, jnp.zeros((), jnp.float32))
    stacked = jnp.concatenate([first_out[None], second_out[None], others], axis=0)
    return jnp.transpose(stacked, (1, 2, 0)).reshape(pair_total, block_total, 2, 128)

def reference(sky_map, noise_weight, prior_weight, seeds, loop_cos, pair_m, block_count):
    block_side, column_m, block_start = block_layout(pair_m, block_count, jnp.arange(NBP, dtype=jnp.int32))
    every_m = pair_m.reshape(NCOL)
    map_scale = 1.0 / math.sqrt(NRING * NPHI)

    def to_map(coef):
        spectra = sum_columns(coef, block_side, column_m, block_start, seeds, loop_cos)
        values = jnp.transpose(spectra[0]) + 1j * jnp.transpose(spectra[1])
        spectrum = jnp.zeros((NRING, NPHI // 2 + 1), values.dtype).at[:, every_m].add(values)
        return jnp.fft.irfft(spectrum, n=NPHI, axis=1) * (NPHI * 0.5 * map_scale)

    def to_coef(pixels):
        spectrum = jnp.fft.rfft(pixels, axis=1)[:, every_m]
        spectra = map_scale * jnp.stack([jnp.transpose(jnp.real(spectrum)), jnp.transpose(jnp.imag(spectrum))])
        return spread_columns(spectra, block_side, column_m, block_start, seeds, loop_cos)

    def operate(coef):
        return prior_weight * coef + to_coef(noise_weight * to_map(coef))
    rhs_coef = to_coef(noise_weight * sky_map)
    solution = jnp.zeros_like(rhs_coef)
    residual = rhs_coef
    direction = rhs_coef
    norm_now = jnp.sum(residual * residual)
    for turn_id in range(ITERS):
        applied = operate(direction)
        step_len = norm_now / jnp.sum(direction * applied)
        solution = solution + step_len * direction
        residual = residual - step_len * applied
        norm_next = jnp.sum(residual * residual)
        direction = residual + norm_next / norm_now * direction
        norm_now = norm_next
    return (solution, residual)
```

```python
import functools
import math

import jax
import jax.numpy as jnp
from jax import lax
from jax.experimental import pallas as pl
from jax.experimental.pallas import tpu as pltpu
from jax.sharding import PartitionSpec as P

DEG = 128
INNER = 1024
FINE = 32
CHUNK = 8
MESH = pl.DeviceIdType.MESH


def split(x):
    hi = x.astype(jnp.bfloat16)
    return hi, (x - hi.astype(jnp.float32)).astype(jnp.bfloat16)


def kernel(
    nb, scale,
    sky, noise, prior, seeds, lcos, coef_a, coef_b, side,
    cos_a, sin_a, cos_b, sin_b, cos_o, sin_o,
    sol, res,
    legendre, basis_hi, basis_lo, pix_hi, pix_lo, st_hi, st_lo, vecs, send, recv, send_sem, recv_sem,
):
    rows, width = sky.shape
    outer = width // INNER
    cols = cos_o.shape[1]
    pairs = cols // 2
    rings = lcos.shape[1]
    groups = rings // 128
    per = 128 // rows
    n = 2 * nb
    k = lax.axis_index("blk")
    c = lax.axis_index("rep")
    me = c * nb + k
    chunk_rows = CHUNK * rows

    def peer_of(d):
        peer = lax.rem(me + d, n)
        return lax.rem(peer, nb), peer // nb

    barrier = pltpu.get_barrier_semaphore()

    def greet(d, _):
        pk, pc = peer_of(d)
        pl.semaphore_signal(barrier, inc=1, device_id=(pk, pc), device_id_type=MESH)
        return 0

    lax.fori_loop(1, n, greet, 0)

    def post(phase, common):
        def one(d, _):
            pk, pc = peer_of(d)
            pltpu.make_async_remote_copy(
                src_ref=send.at[phase, 0 if common else pk],
                dst_ref=recv.at[phase, me],
                send_sem=send_sem.at[phase],
                recv_sem=recv_sem.at[phase],
                device_id=(pk, pc),
                device_id_type=MESH,
            ).start()
            return 0

        lax.fori_loop(1, n, one, 0)
        recv[phase, me] = send[phase, 0 if common else k]

    def drain(phase, sem):
        block = recv.at[phase, pl.ds(0, n - 1)]
        pltpu.make_async_copy(block, block, sem.at[phase]).wait()

    def make_basis(a, _):
        ca, sa = cos_a[pl.ds(a, 1), :], sin_a[pl.ds(a, 1), :]
        cb, sb = cos_b[...], sin_b[...]
        where = pl.ds(pl.multiple_of(a * FINE, FINE), FINE)
        hi, lo = split(ca * cb - sa * sb)
        basis_hi[where, :cols] = hi
        basis_lo[where, :cols] = lo
        hi, lo = split(sa * cb + ca * sb)
        basis_hi[where, cols:] = hi
        basis_lo[where, cols:] = lo
        return 0

    lax.fori_loop(0, INNER // FINE, make_basis, 0)

    def first_pixels(j, _):
        lanes = pl.ds(pl.multiple_of(j * INNER, INNER), INNER)
        hi, lo = split(sky[:, lanes] * noise[:, lanes])
        where = pl.ds(pl.multiple_of(j * rows, rows), rows)
        pix_hi[where, :] = hi
        pix_lo[where, :] = lo
        return 0

    lax.fori_loop(0, outer, first_pixels, 0)
    vecs[0] = jnp.zeros(vecs.shape[1:], jnp.float32)

    def make_legendre():
        x = jnp.broadcast_to(lcos[...][None], (2, 8, rings))
        wide = lambda a: jnp.concatenate([a] * groups, axis=-1)
        p0, p1 = seeds[0], seeds[1]
        legendre[0] = p0
        legendre[1] = p1

        def advance(i, packed):
            earlier, latest = packed
            now = wide(coef_a[i]) * (x * latest - wide(coef_b[i]) * earlier)
            legendre[i] = now
            return latest, now

        lax.fori_loop(2, DEG, advance, (p0, p1))

    def dots(a_hi, a_lo, b_hi, b_lo, dims):
        dot = functools.partial(
            lax.dot_general, dimension_numbers=dims, preferred_element_type=jnp.float32
        )
        return dot(a_hi, b_hi) + (dot(a_hi, b_lo) + dot(a_lo, b_hi))

    def forward(phase):
        def chunk(h, sums):
            re, im = sums
            where = pl.ds(pl.multiple_of(h * chunk_rows, chunk_rows), chunk_rows)
            sect = dots(
                pix_hi[where, :], pix_lo[where, :], basis_hi[...], basis_lo[...],
                (((1,), (0,)), ((), ())),
            )
            for u in range(CHUNK):
                co = cos_o[pl.ds(h * CHUNK + u, 1), :]
                so = sin_o[pl.ds(h * CHUNK + u, 1), :]
                cs = sect[u * rows:(u + 1) * rows, :cols]
                ss = sect[u * rows:(u + 1) * rows, cols:]
                re = re + (cs * co - ss * so)
                im = im - (ss * co + cs * so)
            return re, im

        zero = jnp.zeros((rows, cols), jnp.float32)
        re, im = lax.fori_loop(0, outer // CHUNK, chunk, (zero, zero))
        stacked = scale * jnp.concatenate(
            [re[:, :pairs], im[:, :pairs], re[:, pairs:], im[:, pairs:]], axis=0
        )
        send[phase] = jnp.transpose(stacked).reshape(nb, 8, 128)

    lane = lax.broadcasted_iota(jnp.int32, (8, 128), 1)

    def spread(phase):
        got = [recv[phase, q] + recv[phase, nb + q] for q in range(nb)]
        gathered = []
        for part in range(4):
            at = part * rows
            gathered.append(
                jnp.concatenate([g[:, at:at + rows] for g in got], axis=1)
            )
        spec = {}
        for b in range(2):
            mask = jnp.concatenate([side[b]] * groups, axis=-1) > 0.5
            for t in range(2):
                spec[t, b] = jnp.where(mask, gathered[2 + t], gathered[t])

        def step(g, acc):
            acc = list(acc)
            for u in range(8):
                i = g * 8 + u
                for b in range(2):
                    leg = legendre[i, b]
                    for t in range(2):
                        prod = leg * spec[t, b]
                        tot = prod[:, :128]
                        for q in range(1, groups):
                            tot = tot + prod[:, q * 128:(q + 1) * 128]
                        val = jnp.sum(tot, axis=1, keepdims=True)
                        acc[2 * t + b] = jnp.where(lane == i, val, acc[2 * t + b])
            return tuple(acc)

        zero = jnp.zeros((8, 128), jnp.float32)
        return lax.fori_loop(0, DEG // 8, step, (zero,) * 4)

    def gather_columns(vec, phase):
        def step(g, packed):
            coef, acc = packed
            acc = list(acc)
            for u in range(8):
                for b in range(2):
                    leg = legendre[g * 8 + u, b]
                    for t in range(2):
                        acc[2 * t + b] = acc[2 * t + b] + leg * coef[2 * t + b][:, u:u + 1]
            coef = tuple(pltpu.roll(x, 120, 1) for x in coef)
            return coef, tuple(acc)

        zero = jnp.zeros((8, rings), jnp.float32)
        _, acc = lax.fori_loop(0, DEG // 8, step, (tuple(vec), (zero,) * 4))
        parts = []
        for s in range(2):
            for t in range(2):
                tot = None
                for b in range(2):
                    mask = jnp.concatenate([side[b]] * groups, axis=-1) > 0.5
                    f = acc[2 * t + b]
                    f = jnp.where(mask, f, 0.0) if s else jnp.where(mask, 0.0, f)
                    tot = f if tot is None else tot + f
                parts.append(tot)
        for q in range(nb):
            send[phase, q] = jnp.concatenate(
                [x[:, q * rows:(q + 1) * rows] for x in parts], axis=1
            )

    def inverse(phase):
        table = (recv[phase, pl.ds(0, nb)] + recv[phase, pl.ds(nb, nb)]).reshape(pairs, 128)
        table = scale * jnp.transpose(table)
        re = jnp.concatenate([table[:rows], table[2 * rows:3 * rows]], axis=1)
        im = jnp.concatenate([table[rows:2 * rows], table[3 * rows:]], axis=1)

        def mix(j, _):
            co, so = cos_o[pl.ds(j, 1), :], sin_o[pl.ds(j, 1), :]
            where = pl.ds(pl.multiple_of(j * rows, rows), rows)
            hi, lo = split(re * co - im * so)
            st_hi[where, :cols] = hi
            st_lo[where, :cols] = lo
            hi, lo = split(-(re * so + im * co))
            st_hi[where, cols:] = hi
            st_lo[where, cols:] = lo
            return 0

        lax.fori_loop(0, outer, mix, 0)

        def chunk(h, _):
            where = pl.ds(pl.multiple_of(h * chunk_rows, chunk_rows), chunk_rows)
            pix = dots(
                st_hi[where, :], st_lo[where, :], basis_hi[...], basis_lo[...],
                (((1,), (1,)), ((), ())),
            )
            for u in range(CHUNK):
                j = h * CHUNK + u
                weight = noise[:, pl.ds(pl.multiple_of(j * INNER, INNER), INNER)]
                hi, lo = split(weight * pix[u * rows:(u + 1) * rows])
                at = pl.ds(pl.multiple_of(j * rows, rows), rows)
                pix_hi[at, :] = hi
                pix_lo[at, :] = lo
            return 0

        lax.fori_loop(0, outer // CHUNK, chunk, 0)

    pl.semaphore_wait(barrier, n - 1)

    def turn(it, _):
        forward(2 * it)
        post(2 * it, False)

        @pl.when(it == 0)
        def _():
            make_legendre()

        drain(2 * it, recv_sem)
        out = spread(2 * it)
        vec = []
        for t in range(2):
            for b in range(2):
                vec.append(prior[t, b] * vecs[it, t, b] + out[2 * t + b])
                vecs[it + 1, t, b] = vec[-1]

        @pl.when(it < 2)
        def _():
            gather_columns(vec, 2 * it + 1)
            post(2 * it + 1, False)
            drain(2 * it + 1, recv_sem)
            inverse(2 * it + 1)

        return 0

    lax.fori_loop(0, 3, turn, 0)

    v0, v1, v2 = vecs[1], vecs[2], vecs[3]

    def partial(a, b):
        x = (a * b).reshape(4, 8, 128)
        return jnp.sum(x[0] + x[1] + (x[2] + x[3]), axis=0, keepdims=True)

    send[5, 0] = jnp.concatenate(
        [partial(v0, v0), partial(v0, v1), partial(v1, v1), partial(v0, v2), partial(v1, v2),
         jnp.zeros((3, 128), jnp.float32)], axis=0
    )
    post(5, True)
    drain(5, recv_sem)
    gram = jnp.sum(jnp.sum(recv[5], axis=0), axis=1, keepdims=True)
    bb, bv, vv, bw, vw = (gram[q:q + 1] for q in range(5))
    alpha = bb / bv
    norm = bb - 2.0 * alpha * bv + alpha * alpha * vv
    beta = norm / bb
    more = 1.0 + beta
    curve = more * more * bv - more * alpha * (bw + vv) + alpha * alpha * vw
    alpha2 = norm / curve
    for t in range(2):
        for b in range(2):
            b0, b1, b2 = v0[t, b], v1[t, b], v2[t, b]
            r1 = b0 - alpha * b1
            d1 = r1 + beta * b0
            sol[t, b] = alpha * b0 + alpha2 * d1
            res[t, b] = r1 - alpha2 * (more * b1 - alpha * b2)

    def finish(phase, _):
        drain(phase, send_sem)
        return 0

    lax.fori_loop(0, 6, finish, 0)


def ladder(degree, column_m):
    degree_f = degree.astype(jnp.float32)
    m_over_l = column_m.astype(jnp.float32) / degree_f
    return jnp.sqrt((4.0 - 1.0 / (degree_f * degree_f)) / ((1.0 - m_over_l) * (1.0 + m_over_l)))


def phases(every_m, positions, period):
    cycles = positions[:, None] * every_m[None, :]
    if period & (period - 1) == 0:
        cycles = cycles & (period - 1)
    else:
        cycles = cycles % period
    angles = cycles.astype(jnp.float32) * (2.0 * math.pi / period)
    return jnp.cos(angles), jnp.sin(angles)


def shards(sky_map, noise_weight, prior_weight, seeds, loop_cos, pair_m, block_count):
    nb = lax.axis_size("blk")
    pairs_dev = block_count.shape[0]
    half = seeds.shape[1]
    rings = loop_cos.shape[0]
    cols = 2 * pair_m.shape[0]
    rows, width = sky_map.shape
    period = width * lax.axis_size("rep")
    scale = 1.0 / math.sqrt(rings * period)
    rep = lax.axis_index("rep")
    local_m = lax.dynamic_slice_in_dim(pair_m, lax.axis_index("blk") * pairs_dev, pairs_dev, 0)
    ids = rep * half + jnp.arange(half, dtype=jnp.int32)[:, None]
    on_second = ids >= block_count[None, :]
    offset = jnp.where(on_second, ids - block_count[None, :], ids)
    column_m = jnp.where(on_second, local_m[None, :, 1], local_m[None, :, 0])
    start = 128 * (17 * column_m // 2048 + 1) + 128 * offset
    degree = start[None] + jnp.arange(DEG, dtype=jnp.int32)[:, None, None]
    big = (DEG, half, pairs_dev, 128)
    coef_a = jnp.broadcast_to(ladder(degree, column_m[None])[..., None], big)
    coef_b = jnp.broadcast_to((1.0 / ladder(degree - 1, column_m[None]))[..., None], big)
    side = jnp.broadcast_to(on_second.astype(jnp.float32)[..., None], big[1:])
    every_m = jnp.transpose(pair_m).reshape(cols)
    outer = width // INNER
    coarse = INNER // FINE
    fine_at = jnp.arange(FINE, dtype=jnp.int32)
    coarse_at = FINE * jnp.arange(coarse, dtype=jnp.int32)
    outer_at = rep * width + INNER * jnp.arange(outer, dtype=jnp.int32)
    cos_all, sin_all = phases(every_m, jnp.concatenate([coarse_at, fine_at, outer_at]), period)
    cut = lambda a: (a[:coarse], a[coarse:coarse + FINE], a[coarse + FINE:])
    cos_a, cos_b, cos_o = cut(cos_all)
    sin_a, sin_b, sin_o = cut(sin_all)
    vmem = pl.BlockSpec(memory_space=pltpu.VMEM)
    out = jax.ShapeDtypeStruct((2, half, pairs_dev, DEG), jnp.float32)
    sol, res = pl.pallas_call(
        functools.partial(kernel, nb, scale),
        out_shape=(out, out),
        in_specs=[vmem] * 14,
        out_specs=(vmem, vmem),
        scratch_shapes=[
            pltpu.VMEM((DEG, half, pairs_dev, rings), jnp.float32),
            pltpu.VMEM((INNER, 2 * cols), jnp.bfloat16),
            pltpu.VMEM((INNER, 2 * cols), jnp.bfloat16),
            pltpu.VMEM((outer * rows, INNER), jnp.bfloat16),
            pltpu.VMEM((outer * rows, INNER), jnp.bfloat16),
            pltpu.VMEM((outer * rows, 2 * cols), jnp.bfloat16),
            pltpu.VMEM((outer * rows, 2 * cols), jnp.bfloat16),
            pltpu.VMEM((4, 2, half, pairs_dev, DEG), jnp.float32),
            pltpu.VMEM((6, nb, 8, 128), jnp.float32),
            pltpu.VMEM((6, 2 * nb, 8, 128), jnp.float32),
            pltpu.SemaphoreType.DMA((6,)),
            pltpu.SemaphoreType.DMA((6,)),
        ],
        compiler_params=pltpu.CompilerParams(
            collective_id=0, has_side_effects=True, vmem_limit_bytes=58 * 2**20
        ),
        name="wiener",
    )(
        sky_map, noise_weight,
        jnp.transpose(prior_weight, (2, 1, 0, 3)),
        jnp.transpose(seeds, (2, 1, 0, 3)),
        loop_cos[None, :],
        coef_a, coef_b, side, cos_a, sin_a, cos_b, sin_b, cos_o, sin_o,
    )
    back = lambda a: jnp.transpose(a, (2, 1, 0, 3))
    return back(sol), back(res)


def solution(mesh):
    placed = (
        P("blk", "rep"),
        P("blk", "rep"),
        P("blk", "rep", None, None),
        P("blk", "rep", None, None),
        P(),
        P(),
        P("blk"),
    )
    return jax.shard_map(
        shards,
        mesh=mesh,
        in_specs=placed,
        out_specs=(P("blk", "rep", None, None), P("blk", "rep", None, None)),
        check_vma=False,
    )
```

```python
import functools
import math

import jax
import jax.numpy as jnp
from jax import lax
from jax.experimental import pallas as pl
from jax.experimental.pallas import tpu as pltpu
from jax.sharding import PartitionSpec as P

DEG = 128
INNER = 1024
FINE = 32
CHUNK = 8
MESH = pl.DeviceIdType.MESH


def split(x):
    hi = x.astype(jnp.bfloat16)
    return hi, (x - hi.astype(jnp.float32)).astype(jnp.bfloat16)


def kernel(
    nb, scale, period,
    sky_in, noise_in, prior_in, seeds, lcos, every_m, counts,
    sol, res,
    sky, noise, legendre, basis_hi, basis_lo, pix_hi, pix_lo, st_hi, st_lo,
    cos_a, sin_a, cos_b, sin_b, cos_o, sin_o, by_pair, side, prior,
    vecs, send, recv, load_sem, send_sem, recv_sem,
):
    rows, width = sky.shape
    outer = width // INNER
    cols = cos_o.shape[1]
    pairs = cols // 2
    half = side.shape[0]
    rings = lcos.shape[1]
    groups = rings // 128
    per = 128 // rows
    n = 2 * nb
    k = lax.axis_index("blk")
    c = lax.axis_index("rep")
    me = c * nb + k
    chunk_rows = CHUNK * rows

    def peer_of(d):
        peer = lax.rem(me + d, n)
        return lax.rem(peer, nb), peer // nb

    loads = [
        pltpu.make_async_copy(sky_in, sky, load_sem.at[0]),
        pltpu.make_async_copy(noise_in, noise, load_sem.at[1]),
    ]
    for load in loads:
        load.start()
    barrier = pltpu.get_barrier_semaphore()

    def greet(d, _):
        pk, pc = peer_of(d)
        pl.semaphore_signal(barrier, inc=1, device_id=(pk, pc), device_id_type=MESH)
        return 0

    lax.fori_loop(1, n, greet, 0)

    def post(phase, common):
        def one(d, _):
            pk, pc = peer_of(d)
            pltpu.make_async_remote_copy(
                src_ref=send.at[phase, 0 if common else pk],
                dst_ref=recv.at[phase, me],
                send_sem=send_sem.at[phase],
                recv_sem=recv_sem.at[phase],
                device_id=(pk, pc),
                device_id_type=MESH,
            ).start()
            return 0

        lax.fori_loop(1, n, one, 0)
        recv[phase, me] = send[phase, 0 if common else k]

    def drain(phase, sem):
        block = recv.at[phase, pl.ds(0, n - 1)]
        pltpu.make_async_copy(block, block, sem.at[phase]).wait()

    m_row = jnp.concatenate([every_m[0:1, :], every_m[1:2, :]], axis=1)

    def trig(count, base, step, cos_ref, sin_ref):
        at = base + step * lax.broadcasted_iota(jnp.int32, (count, cols), 0)
        cos_ref[...], sin_ref[...] = phases(at * m_row, period)

    trig(INNER // FINE, 0, FINE, cos_a, sin_a)
    trig(FINE, 0, 1, cos_b, sin_b)
    trig(outer, c * width, INNER, cos_o, sin_o)

    def make_basis(a, _):
        ca, sa = cos_a[pl.ds(a, 1), :], sin_a[pl.ds(a, 1), :]
        cb, sb = cos_b[...], sin_b[...]
        where = pl.ds(pl.multiple_of(a * FINE, FINE), FINE)
        hi, lo = split(ca * cb - sa * sb)
        basis_hi[where, :cols] = hi
        basis_lo[where, :cols] = lo
        hi, lo = split(sa * cb + ca * sb)
        basis_hi[where, cols:] = hi
        basis_lo[where, cols:] = lo
        return 0

    lax.fori_loop(0, INNER // FINE, make_basis, 0)

    for load in loads:
        load.wait()

    def first_pixels(j, _):
        lanes = pl.ds(pl.multiple_of(j * INNER, INNER), INNER)
        hi, lo = split(sky[:, lanes] * noise[:, lanes])
        where = pl.ds(pl.multiple_of(j * rows, rows), rows)
        pix_hi[where, :] = hi
        pix_lo[where, :] = lo
        return 0

    lax.fori_loop(0, outer, first_pixels, 0)
    vecs[0] = jnp.zeros(vecs.shape[1:], jnp.float32)

    row_id = lax.broadcasted_iota(jnp.int32, (8, 128), 0)
    lane = lax.broadcasted_iota(jnp.int32, (8, 128), 1)

    def make_legendre():
        m_float = every_m[...].astype(jnp.float32)
        by_pair[...] = jnp.transpose(
            jnp.concatenate([m_float, jnp.zeros((126, pairs), jnp.float32)], axis=0)
        )
        mine = by_pair[pl.ds(pl.multiple_of(k * 8, 8), 8), :]
        m_first = jnp.broadcast_to(mine[:, 0:1], (8, 128)).astype(jnp.int32)
        m_second = jnp.broadcast_to(mine[:, 1:2], (8, 128)).astype(jnp.int32)
        count = jnp.zeros((8, 128), jnp.int32)
        for p in range(8):
            count = jnp.where(row_id == p, counts[p], count)
        coefs = []
        for b in range(half):
            block = c * half + b
            second = count <= block
            offset = jnp.where(second, block - count, block)
            column = jnp.where(second, m_second, m_first)
            degree = 128 * (lax.shift_right_logical(17 * column, 11) + 1) + 128 * offset + lane
            coefs.append((ladder(degree, column), 1.0 / ladder(degree - 1, column)))
            side[b] = jnp.where(second, 1.0, 0.0)
            for t in range(2):
                prior[t, b] = jnp.concatenate(
                    [prior_in[p, b, t:t + 1, :] for p in range(8)], axis=0
                )
        x = jnp.broadcast_to(lcos[...], (8, rings))
        wide = lambda a, u: jnp.concatenate(
            [jnp.broadcast_to(a[:, u:u + 1], (8, 128))] * groups, axis=-1
        )
        state = []
        for b in range(half):
            for i in range(2):
                state.append(
                    jnp.concatenate([seeds[p, b, i:i + 1, :] for p in range(8)], axis=0)
                )
                legendre[i, b] = state[-1]

        def advance(i, u, coefs, state):
            out = []
            for b in range(half):
                earlier, latest = state[2 * b:2 * b + 2]
                ca, cb = coefs[2 * b:2 * b + 2]
                now = wide(ca, u) * (x * latest - wide(cb, u) * earlier)
                legendre[i, b] = now
                out += [latest, now]
            return out

        coefs = [v for pair in coefs for v in pair]
        for i in range(2, 8):
            state = advance(i, i, coefs, state)

        def step(g, packed):
            coefs, state = packed
            coefs = tuple(pltpu.roll(v, 120, 1) for v in coefs)
            for u in range(8):
                state = advance(g * 8 + u, u, coefs, state)
            return coefs, tuple(state)

        lax.fori_loop(1, DEG // 8, step, (tuple(coefs), tuple(state)))

    def dots(a_hi, a_lo, b_hi, b_lo, dims):
        dot = functools.partial(
            lax.dot_general, dimension_numbers=dims, preferred_element_type=jnp.float32
        )
        return dot(a_hi, b_hi) + (dot(a_hi, b_lo) + dot(a_lo, b_hi))

    def forward(phase):
        def chunk(h, sums):
            re, im = sums
            where = pl.ds(pl.multiple_of(h * chunk_rows, chunk_rows), chunk_rows)
            sect = dots(
                pix_hi[where, :], pix_lo[where, :], basis_hi[...], basis_lo[...],
                (((1,), (0,)), ((), ())),
            )
            for u in range(CHUNK):
                co = cos_o[pl.ds(h * CHUNK + u, 1), :]
                so = sin_o[pl.ds(h * CHUNK + u, 1), :]
                cs = sect[u * rows:(u + 1) * rows, :cols]
                ss = sect[u * rows:(u + 1) * rows, cols:]
                re = re + (cs * co - ss * so)
                im = im - (ss * co + cs * so)
            return re, im

        zero = jnp.zeros((rows, cols), jnp.float32)
        re, im = lax.fori_loop(0, outer // CHUNK, chunk, (zero, zero))
        stacked = scale * jnp.concatenate(
            [re[:, :pairs], im[:, :pairs], re[:, pairs:], im[:, pairs:]], axis=0
        )
        send[phase] = jnp.transpose(stacked).reshape(nb, 8, 128)

    def spread(phase):
        got = [recv[phase, q] + recv[phase, nb + q] for q in range(nb)]
        gathered = []
        for part in range(4):
            at = part * rows
            gathered.append(
                jnp.concatenate([g[:, at:at + rows] for g in got], axis=1)
            )
        spec = {}
        for b in range(2):
            mask = jnp.concatenate([side[b]] * groups, axis=-1) > 0.5
            for t in range(2):
                spec[t, b] = jnp.where(mask, gathered[2 + t], gathered[t])

        def step(g, acc):
            acc = list(acc)
            for u in range(8):
                i = g * 8 + u
                for b in range(2):
                    leg = legendre[i, b]
                    for t in range(2):
                        prod = leg * spec[t, b]
                        tot = prod[:, :128]
                        for q in range(1, groups):
                            tot = tot + prod[:, q * 128:(q + 1) * 128]
                        val = jnp.sum(tot, axis=1, keepdims=True)
                        acc[2 * t + b] = jnp.where(lane == i, val, acc[2 * t + b])
            return tuple(acc)

        zero = jnp.zeros((8, 128), jnp.float32)
        return lax.fori_loop(0, DEG // 8, step, (zero,) * 4)

    def gather_columns(vec, phase):
        def step(g, packed):
            coef, acc = packed
            acc = list(acc)
            for u in range(8):
                for b in range(2):
                    leg = legendre[g * 8 + u, b]
                    for t in range(2):
                        acc[2 * t + b] = acc[2 * t + b] + leg * coef[2 * t + b][:, u:u + 1]
            coef = tuple(pltpu.roll(x, 120, 1) for x in coef)
            return coef, tuple(acc)

        zero = jnp.zeros((8, rings), jnp.float32)
        _, acc = lax.fori_loop(0, DEG // 8, step, (tuple(vec), (zero,) * 4))
        parts = []
        for s in range(2):
            for t in range(2):
                tot = None
                for b in range(2):
                    mask = jnp.concatenate([side[b]] * groups, axis=-1) > 0.5
                    f = acc[2 * t + b]
                    f = jnp.where(mask, f, 0.0) if s else jnp.where(mask, 0.0, f)
                    tot = f if tot is None else tot + f
                parts.append(tot)
        for q in range(nb):
            send[phase, q] = jnp.concatenate(
                [x[:, q * rows:(q + 1) * rows] for x in parts], axis=1
            )

    def inverse(phase):
        table = (recv[phase, pl.ds(0, nb)] + recv[phase, pl.ds(nb, nb)]).reshape(pairs, 128)
        table = scale * jnp.transpose(table)
        re = jnp.concatenate([table[:rows], table[2 * rows:3 * rows]], axis=1)
        im = jnp.concatenate([table[rows:2 * rows], table[3 * rows:]], axis=1)

        def mix(j, _):
            co, so = cos_o[pl.ds(j, 1), :], sin_o[pl.ds(j, 1), :]
            where = pl.ds(pl.multiple_of(j * rows, rows), rows)
            hi, lo = split(re * co - im * so)
            st_hi[where, :cols] = hi
            st_lo[where, :cols] = lo
            hi, lo = split(-(re * so + im * co))
            st_hi[where, cols:] = hi
            st_lo[where, cols:] = lo
            return 0

        lax.fori_loop(0, outer, mix, 0)

        def chunk(h, energy):
            where = pl.ds(pl.multiple_of(h * chunk_rows, chunk_rows), chunk_rows)
            pix = dots(
                st_hi[where, :], st_lo[where, :], basis_hi[...], basis_lo[...],
                (((1,), (1,)), ((), ())),
            )
            for u in range(CHUNK):
                j = h * CHUNK + u
                weight = noise[:, pl.ds(pl.multiple_of(j * INNER, INNER), INNER)]
                values = pix[u * rows:(u + 1) * rows]
                weighted = weight * values
                power = weighted * values
                for q in range(INNER // 128):
                    energy = energy + power[:, q * 128:(q + 1) * 128]
                hi, lo = split(weighted)
                at = pl.ds(pl.multiple_of(j * rows, rows), rows)
                pix_hi[at, :] = hi
                pix_lo[at, :] = lo
            return energy

        return lax.fori_loop(0, outer // CHUNK, chunk, jnp.zeros((rows, 128), jnp.float32))

    def dot_lanes(a, b):
        x = (a * b).reshape(4, 8, 128)
        return jnp.sum(x[0] + x[1] + (x[2] + x[3]), axis=0, keepdims=True)

    pl.semaphore_wait(barrier, n - 1)

    def turn(it, _):
        forward(2 * it)
        post(2 * it, False)

        @pl.when(it == 0)
        def _():
            make_legendre()

        drain(2 * it, recv_sem)
        out = spread(2 * it)
        vec = []
        for t in range(2):
            for b in range(2):
                vec.append(prior[t, b] * vecs[it, t, b] + out[2 * t + b])
                vecs[it + 1, t, b] = vec[-1]

        @pl.when(it < 2)
        def _():
            gather_columns(vec, 2 * it + 1)
            post(2 * it + 1, False)
            drain(2 * it + 1, recv_sem)
            energy = inverse(2 * it + 1)

            @pl.when(it == 1)
            def _():
                v0, v1 = vecs[1], vecs[2]
                bent = dot_lanes(v1, prior[...] * v1) + jnp.sum(energy, axis=0, keepdims=True)
                send[5, 0] = jnp.concatenate(
                    [dot_lanes(v0, v0), dot_lanes(v0, v1), dot_lanes(v1, v1), bent,
                     jnp.zeros((4, 128), jnp.float32)], axis=0
                )
                post(5, True)

        return 0

    lax.fori_loop(0, 3, turn, 0)

    v0, v1, v2 = vecs[1], vecs[2], vecs[3]

    drain(5, recv_sem)
    gram = jnp.sum(jnp.sum(recv[5], axis=0), axis=1, keepdims=True)
    bb, bv, vv, vw = (gram[q:q + 1] for q in range(4))
    alpha = bb / bv
    norm = bb - 2.0 * alpha * bv + alpha * alpha * vv
    beta = norm / bb
    more = 1.0 + beta
    curve = more * more * bv - 2.0 * more * alpha * vv + alpha * alpha * vw
    alpha2 = norm / curve
    for t in range(2):
        for b in range(2):
            b0, b1, b2 = v0[t, b], v1[t, b], v2[t, b]
            r1 = b0 - alpha * b1
            d1 = r1 + beta * b0
            found = alpha * b0 + alpha2 * d1
            left = r1 - alpha2 * (more * b1 - alpha * b2)
            for p in range(8):
                sol[p, b, t:t + 1, :] = found[p:p + 1]
                res[p, b, t:t + 1, :] = left[p:p + 1]

    def finish(phase, _):
        drain(phase, send_sem)
        return 0

    lax.fori_loop(0, 6, finish, 0)


def ladder(degree, column_m):
    degree_f = degree.astype(jnp.float32)
    m_over_l = column_m.astype(jnp.float32) / degree_f
    return jnp.sqrt((4.0 - 1.0 / (degree_f * degree_f)) / ((1.0 - m_over_l) * (1.0 + m_over_l)))


def phases(cycles, period):
    quarter = period // 4
    if period & (period - 1) == 0:
        cycles = cycles & (period - 1)
        turn = lax.shift_right_logical(cycles + quarter // 2, quarter.bit_length() - 1)
    else:
        cycles = lax.rem(cycles, period)
        turn = lax.div(cycles + quarter // 2, quarter)
    x = (cycles - quarter * turn).astype(jnp.float32) * (2.0 * math.pi / period)
    y = x * x
    sin = x * (1 + y * (-1 / 6 + y * (1 / 120 + y * (-1 / 5040 + y * (1 / 362880)))))
    cos = 1 + y * (-1 / 2 + y * (1 / 24 + y * (-1 / 720 + y * (1 / 40320 - y * (1 / 3628800)))))
    odd = (turn & 1) == 1
    cos_abs, sin_abs = jnp.where(odd, sin, cos), jnp.where(odd, cos, sin)
    return (
        jnp.where(((turn + 1) & 2) == 2, -cos_abs, cos_abs),
        jnp.where((turn & 2) == 2, -sin_abs, sin_abs),
    )


def shards(sky_map, noise_weight, prior_weight, seeds, loop_cos, pair_m, block_count):
    nb = lax.axis_size("blk")
    pairs_dev = block_count.shape[0]
    half = seeds.shape[1]
    rings = loop_cos.shape[0]
    pairs = pair_m.shape[0]
    cols = 2 * pairs
    rows, width = sky_map.shape
    period = width * lax.axis_size("rep")
    scale = 1.0 / math.sqrt(rings * period)
    outer = width // INNER
    vmem = pl.BlockSpec(memory_space=pltpu.VMEM)
    hbm = pl.BlockSpec(memory_space=pl.ANY)
    smem = pl.BlockSpec(memory_space=pltpu.SMEM)
    out = jax.ShapeDtypeStruct(prior_weight.shape, jnp.float32)
    f32 = lambda *shape: pltpu.VMEM(shape, jnp.float32)
    b16 = lambda *shape: pltpu.VMEM(shape, jnp.bfloat16)
    return pl.pallas_call(
        functools.partial(kernel, nb, scale, period),
        out_shape=(out, out),
        in_specs=[hbm, hbm, vmem, vmem, vmem, vmem, smem],
        out_specs=(vmem, vmem),
        scratch_shapes=[
            f32(rows, width),
            f32(rows, width),
            f32(DEG, half, pairs_dev, rings),
            b16(INNER, 2 * cols),
            b16(INNER, 2 * cols),
            b16(outer * rows, INNER),
            b16(outer * rows, INNER),
            b16(outer * rows, 2 * cols),
            b16(outer * rows, 2 * cols),
            f32(INNER // FINE, cols),
            f32(INNER // FINE, cols),
            f32(FINE, cols),
            f32(FINE, cols),
            f32(outer, cols),
            f32(outer, cols),
            f32(pairs, 128),
            f32(half, pairs_dev, 128),
            f32(2, half, pairs_dev, DEG),
            f32(4, 2, half, pairs_dev, DEG),
            f32(6, nb, 8, 128),
            f32(6, 2 * nb, 8, 128),
            pltpu.SemaphoreType.DMA((2,)),
            pltpu.SemaphoreType.DMA((6,)),
            pltpu.SemaphoreType.DMA((6,)),
        ],
        compiler_params=pltpu.CompilerParams(
            collective_id=0, has_side_effects=True, vmem_limit_bytes=58 * 2**20
        ),
        name="wiener",
    )(
        sky_map, noise_weight, prior_weight, seeds, loop_cos[None, :],
        jnp.transpose(pair_m), block_count,
    )


def solution(mesh):
    placed = (
        P("blk", "rep"),
        P("blk", "rep"),
        P("blk", "rep", None, None),
        P("blk", "rep", None, None),
        P(),
        P(),
        P("blk"),
    )
    return jax.shard_map(
        shards,
        mesh=mesh,
        in_specs=placed,
        out_specs=(P("blk", "rep", None, None), P("blk", "rep", None, None)),
        check_vma=False,
    )
```

```python
import functools
import math

import jax
import jax.numpy as jnp
from jax import lax
from jax.experimental import pallas as pl
from jax.experimental.pallas import tpu as pltpu
from jax.sharding import PartitionSpec as P

DEG = 128
INNER = 1024
FINE = 32
CHUNK = 8
MESH = pl.DeviceIdType.MESH


def split(x):
    hi = x.astype(jnp.bfloat16)
    return hi, (x - hi.astype(jnp.float32)).astype(jnp.bfloat16)


def kernel(
    nb, scale, period,
    sky_in, noise_in, prior_in, seeds, lcos, every_m, counts,
    sol, res,
    sky, noise, legendre, basis_hi, basis_lo, pix_hi, pix_lo, st_hi, st_lo,
    cos_a, sin_a, cos_b, sin_b, cos_o, sin_o, by_pair, side, prior,
    vecs, send, recv, load_sem, send_sem, recv_sem,
):
    rows, width = sky.shape
    outer = width // INNER
    cols = cos_o.shape[1]
    pairs = cols // 2
    half = side.shape[0]
    rings = lcos.shape[1]
    groups = rings // 128
    per = 128 // rows
    n = 2 * nb
    k = lax.axis_index("blk")
    c = lax.axis_index("rep")
    me = c * nb + k
    chunk_rows = CHUNK * rows

    def peer_of(d):
        peer = lax.rem(me + d, n)
        return lax.rem(peer, nb), peer // nb

    loads = [
        pltpu.make_async_copy(sky_in, sky, load_sem.at[0]),
        pltpu.make_async_copy(noise_in, noise, load_sem.at[1]),
    ]
    for load in loads:
        load.start()
    barrier = pltpu.get_barrier_semaphore()

    def greet(d, _):
        pk, pc = peer_of(d)
        pl.semaphore_signal(barrier, inc=1, device_id=(pk, pc), device_id_type=MESH)
        return 0

    lax.fori_loop(1, n, greet, 0)

    def post(phase, common):
        def one(d, _):
            pk, pc = peer_of(d)
            pltpu.make_async_remote_copy(
                src_ref=send.at[phase, 0 if common else pk],
                dst_ref=recv.at[phase, me],
                send_sem=send_sem.at[phase],
                recv_sem=recv_sem.at[phase],
                device_id=(pk, pc),
                device_id_type=MESH,
            ).start()
            return 0

        lax.fori_loop(1, n, one, 0)
        recv[phase, me] = send[phase, 0 if common else k]

    def drain(phase, sem):
        block = recv.at[phase, pl.ds(0, n - 1)]
        pltpu.make_async_copy(block, block, sem.at[phase]).wait()

    m_row = jnp.concatenate([every_m[0:1, :], every_m[1:2, :]], axis=1)

    def trig(count, base, step, cos_ref, sin_ref):
        at = base + step * lax.broadcasted_iota(jnp.int32, (count, cols), 0)
        cos_ref[...], sin_ref[...] = phases(at * m_row, period)

    trig(INNER // FINE, 0, FINE, cos_a, sin_a)
    trig(FINE, 0, 1, cos_b, sin_b)
    trig(outer, c * width, INNER, cos_o, sin_o)

    def make_basis(a, _):
        ca, sa = cos_a[pl.ds(a, 1), :], sin_a[pl.ds(a, 1), :]
        cb, sb = cos_b[...], sin_b[...]
        where = pl.ds(pl.multiple_of(a * FINE, FINE), FINE)
        hi, lo = split(ca * cb - sa * sb)
        basis_hi[where, :cols] = hi
        basis_lo[where, :cols] = lo
        hi, lo = split(sa * cb + ca * sb)
        basis_hi[where, cols:] = hi
        basis_lo[where, cols:] = lo
        return 0

    lax.fori_loop(0, INNER // FINE, make_basis, 0)

    for load in loads:
        load.wait()

    def first_pixels(j, _):
        lanes = pl.ds(pl.multiple_of(j * INNER, INNER), INNER)
        hi, lo = split(sky[:, lanes] * noise[:, lanes])
        where = pl.ds(pl.multiple_of(j * rows, rows), rows)
        pix_hi[where, :] = hi
        pix_lo[where, :] = lo
        return 0

    lax.fori_loop(0, outer, first_pixels, 0)
    vecs[0] = jnp.zeros(vecs.shape[1:], jnp.float32)

    row_id = lax.broadcasted_iota(jnp.int32, (8, 128), 0)
    lane = lax.broadcasted_iota(jnp.int32, (8, 128), 1)

    def make_legendre():
        m_float = every_m[...].astype(jnp.float32)
        by_pair[...] = jnp.transpose(
            jnp.concatenate([m_float, jnp.zeros((126, pairs), jnp.float32)], axis=0)
        )
        mine = by_pair[pl.ds(pl.multiple_of(k * 8, 8), 8), :]
        m_first = jnp.broadcast_to(mine[:, 0:1], (8, 128)).astype(jnp.int32)
        m_second = jnp.broadcast_to(mine[:, 1:2], (8, 128)).astype(jnp.int32)
        count = jnp.zeros((8, 128), jnp.int32)
        for p in range(8):
            count = jnp.where(row_id == p, counts[p], count)
        coefs = []
        for b in range(half):
            block = c * half + b
            second = count <= block
            offset = jnp.where(second, block - count, block)
            column = jnp.where(second, m_second, m_first)
            degree = 128 * (lax.shift_right_logical(17 * column, 11) + 1) + 128 * offset + lane
            coefs.append((ladder(degree, column), 1.0 / ladder(degree - 1, column)))
            side[b] = jnp.where(second, 1.0, 0.0)
            for t in range(2):
                prior[t, b] = jnp.concatenate(
                    [prior_in[p, b, t:t + 1, :] for p in range(8)], axis=0
                )
        x = jnp.broadcast_to(lcos[...], (8, rings))
        wide = lambda a, u: jnp.concatenate(
            [jnp.broadcast_to(a[:, u:u + 1], (8, 128))] * groups, axis=-1
        )
        state = []
        for b in range(half):
            for i in range(2):
                state.append(
                    jnp.concatenate([seeds[p, b, i:i + 1, :] for p in range(8)], axis=0)
                )
                legendre[i, b] = state[-1]

        def advance(i, u, coefs, state):
            out = []
            for b in range(half):
                earlier, latest = state[2 * b:2 * b + 2]
                ca, cb = coefs[2 * b:2 * b + 2]
                now = wide(ca, u) * (x * latest - wide(cb, u) * earlier)
                legendre[i, b] = now
                out += [latest, now]
            return out

        coefs = [v for pair in coefs for v in pair]
        for i in range(2, 8):
            state = advance(i, i, coefs, state)

        def step(g, packed):
            coefs, state = packed
            coefs = tuple(pltpu.roll(v, 120, 1) for v in coefs)
            for u in range(8):
                state = advance(g * 8 + u, u, coefs, state)
            return coefs, tuple(state)

        lax.fori_loop(1, DEG // 8, step, (tuple(coefs), tuple(state)))

    def dots(a_hi, a_lo, b_hi, b_lo, dims):
        dot = functools.partial(
            lax.dot_general, dimension_numbers=dims, preferred_element_type=jnp.float32
        )
        both = dot(jnp.concatenate([a_hi, a_lo], axis=0), b_hi)
        size = a_hi.shape[0]
        return both[:size] + (both[size:] + dot(a_hi, b_lo))

    def forward(phase):
        def chunk(h, sums):
            re, im = sums
            where = pl.ds(pl.multiple_of(h * chunk_rows, chunk_rows), chunk_rows)
            sect = dots(
                pix_hi[where, :], pix_lo[where, :], basis_hi[...], basis_lo[...],
                (((1,), (0,)), ((), ())),
            )
            for u in range(CHUNK):
                co = cos_o[pl.ds(h * CHUNK + u, 1), :]
                so = sin_o[pl.ds(h * CHUNK + u, 1), :]
                cs = sect[u * rows:(u + 1) * rows, :cols]
                ss = sect[u * rows:(u + 1) * rows, cols:]
                re = re + (cs * co - ss * so)
                im = im - (ss * co + cs * so)
            return re, im

        zero = jnp.zeros((rows, cols), jnp.float32)
        re, im = lax.fori_loop(0, outer // CHUNK, chunk, (zero, zero))
        stacked = scale * jnp.concatenate(
            [re[:, :pairs], im[:, :pairs], re[:, pairs:], im[:, pairs:]], axis=0
        )
        send[phase] = jnp.transpose(stacked).reshape(nb, 8, 128)

    def spread(phase):
        got = [recv[phase, q] + recv[phase, nb + q] for q in range(nb)]
        gathered = []
        for part in range(4):
            at = part * rows
            gathered.append(
                jnp.concatenate([g[:, at:at + rows] for g in got], axis=1)
            )
        spec = {}
        for b in range(2):
            mask = jnp.concatenate([side[b]] * groups, axis=-1) > 0.5
            for t in range(2):
                spec[t, b] = jnp.where(mask, gathered[2 + t], gathered[t])

        def step(g, acc):
            acc = list(acc)
            for u in range(8):
                i = g * 8 + u
                for b in range(2):
                    leg = legendre[i, b]
                    for t in range(2):
                        prod = leg * spec[t, b]
                        tot = prod[:, :128]
                        for q in range(1, groups):
                            tot = tot + prod[:, q * 128:(q + 1) * 128]
                        val = jnp.sum(tot, axis=1, keepdims=True)
                        acc[2 * t + b] = jnp.where(lane == i, val, acc[2 * t + b])
            return tuple(acc)

        zero = jnp.zeros((8, 128), jnp.float32)
        return lax.fori_loop(0, DEG // 8, step, (zero,) * 4)

    def gather_columns(vec, phase):
        def step(g, packed):
            coef, acc = packed
            acc = list(acc)
            for u in range(8):
                for b in range(2):
                    leg = legendre[g * 8 + u, b]
                    for t in range(2):
                        acc[2 * t + b] = acc[2 * t + b] + leg * coef[2 * t + b][:, u:u + 1]
            coef = tuple(pltpu.roll(x, 120, 1) for x in coef)
            return coef, tuple(acc)

        zero = jnp.zeros((8, rings), jnp.float32)
        _, acc = lax.fori_loop(0, DEG // 8, step, (tuple(vec), (zero,) * 4))
        parts = []
        for s in range(2):
            for t in range(2):
                tot = None
                for b in range(2):
                    mask = jnp.concatenate([side[b]] * groups, axis=-1) > 0.5
                    f = acc[2 * t + b]
                    f = jnp.where(mask, f, 0.0) if s else jnp.where(mask, 0.0, f)
                    tot = f if tot is None else tot + f
                parts.append(tot)
        for q in range(nb):
            send[phase, q] = jnp.concatenate(
                [x[:, q * rows:(q + 1) * rows] for x in parts], axis=1
            )

    def inverse(phase):
        table = (recv[phase, pl.ds(0, nb)] + recv[phase, pl.ds(nb, nb)]).reshape(pairs, 128)
        table = scale * jnp.transpose(table)
        re = jnp.concatenate([table[:rows], table[2 * rows:3 * rows]], axis=1)
        im = jnp.concatenate([table[rows:2 * rows], table[3 * rows:]], axis=1)

        def mix(j, _):
            co, so = cos_o[pl.ds(j, 1), :], sin_o[pl.ds(j, 1), :]
            where = pl.ds(pl.multiple_of(j * rows, rows), rows)
            hi, lo = split(re * co - im * so)
            st_hi[where, :cols] = hi
            st_lo[where, :cols] = lo
            hi, lo = split(-(re * so + im * co))
            st_hi[where, cols:] = hi
            st_lo[where, cols:] = lo
            return 0

        lax.fori_loop(0, outer, mix, 0)

        def chunk(h, energy):
            where = pl.ds(pl.multiple_of(h * chunk_rows, chunk_rows), chunk_rows)
            pix = dots(
                st_hi[where, :], st_lo[where, :], basis_hi[...], basis_lo[...],
                (((1,), (1,)), ((), ())),
            )
            for u in range(CHUNK):
                j = h * CHUNK + u
                weight = noise[:, pl.ds(pl.multiple_of(j * INNER, INNER), INNER)]
                values = pix[u * rows:(u + 1) * rows]
                weighted = weight * values
                power = weighted * values
                for q in range(INNER // 128):
                    energy = energy + power[:, q * 128:(q + 1) * 128]
                hi, lo = split(weighted)
                at = pl.ds(pl.multiple_of(j * rows, rows), rows)
                pix_hi[at, :] = hi
                pix_lo[at, :] = lo
            return energy

        return lax.fori_loop(0, outer // CHUNK, chunk, jnp.zeros((rows, 128), jnp.float32))

    def dot_lanes(a, b):
        x = (a * b).reshape(4, 8, 128)
        return jnp.sum(x[0] + x[1] + (x[2] + x[3]), axis=0, keepdims=True)

    pl.semaphore_wait(barrier, n - 1)

    def turn(it, _):
        forward(2 * it)
        post(2 * it, False)

        @pl.when(it == 0)
        def _():
            make_legendre()

        drain(2 * it, recv_sem)
        out = spread(2 * it)
        vec = []
        for t in range(2):
            for b in range(2):
                vec.append(prior[t, b] * vecs[it, t, b] + out[2 * t + b])
                vecs[it + 1, t, b] = vec[-1]

        @pl.when(it < 2)
        def _():
            gather_columns(vec, 2 * it + 1)
            post(2 * it + 1, False)
            drain(2 * it + 1, recv_sem)
            energy = inverse(2 * it + 1)

            @pl.when(it == 1)
            def _():
                v0, v1 = vecs[1], vecs[2]
                bent = dot_lanes(v1, prior[...] * v1) + jnp.sum(energy, axis=0, keepdims=True)
                send[5, 0] = jnp.concatenate(
                    [dot_lanes(v0, v0), dot_lanes(v0, v1), dot_lanes(v1, v1), bent,
                     jnp.zeros((4, 128), jnp.float32)], axis=0
                )
                post(5, True)

        return 0

    lax.fori_loop(0, 3, turn, 0)

    v0, v1, v2 = vecs[1], vecs[2], vecs[3]

    drain(5, recv_sem)
    gram = jnp.sum(jnp.sum(recv[5], axis=0), axis=1, keepdims=True)
    bb, bv, vv, vw = (gram[q:q + 1] for q in range(4))
    alpha = bb / bv
    norm = bb - 2.0 * alpha * bv + alpha * alpha * vv
    beta = norm / bb
    more = 1.0 + beta
    curve = more * more * bv - 2.0 * more * alpha * vv + alpha * alpha * vw
    alpha2 = norm / curve
    for t in range(2):
        for b in range(2):
            b0, b1, b2 = v0[t, b], v1[t, b], v2[t, b]
            r1 = b0 - alpha * b1
            d1 = r1 + beta * b0
            found = alpha * b0 + alpha2 * d1
            left = r1 - alpha2 * (more * b1 - alpha * b2)
            for p in range(8):
                sol[p, b, t:t + 1, :] = found[p:p + 1]
                res[p, b, t:t + 1, :] = left[p:p + 1]

    def finish(phase, _):
        drain(phase, send_sem)
        return 0

    lax.fori_loop(0, 6, finish, 0)


def ladder(degree, column_m):
    degree_f = degree.astype(jnp.float32)
    m_over_l = column_m.astype(jnp.float32) / degree_f
    return jnp.sqrt((4.0 - 1.0 / (degree_f * degree_f)) / ((1.0 - m_over_l) * (1.0 + m_over_l)))


def phases(cycles, period):
    quarter = period // 4
    if period & (period - 1) == 0:
        cycles = cycles & (period - 1)
        turn = lax.shift_right_logical(cycles + quarter // 2, quarter.bit_length() - 1)
    else:
        cycles = lax.rem(cycles, period)
        turn = lax.div(cycles + quarter // 2, quarter)
    x = (cycles - quarter * turn).astype(jnp.float32) * (2.0 * math.pi / period)
    y = x * x
    sin = x * (1 + y * (-1 / 6 + y * (1 / 120 + y * (-1 / 5040 + y * (1 / 362880)))))
    cos = 1 + y * (-1 / 2 + y * (1 / 24 + y * (-1 / 720 + y * (1 / 40320 - y * (1 / 3628800)))))
    odd = (turn & 1) == 1
    cos_abs, sin_abs = jnp.where(odd, sin, cos), jnp.where(odd, cos, sin)
    return (
        jnp.where(((turn + 1) & 2) == 2, -cos_abs, cos_abs),
        jnp.where((turn & 2) == 2, -sin_abs, sin_abs),
    )


def shards(sky_map, noise_weight, prior_weight, seeds, loop_cos, pair_m, block_count):
    nb = lax.axis_size("blk")
    pairs_dev = block_count.shape[0]
    half = seeds.shape[1]
    rings = loop_cos.shape[0]
    pairs = pair_m.shape[0]
    cols = 2 * pairs
    rows, width = sky_map.shape
    period = width * lax.axis_size("rep")
    scale = 1.0 / math.sqrt(rings * period)
    outer = width // INNER
    vmem = pl.BlockSpec(memory_space=pltpu.VMEM)
    hbm = pl.BlockSpec(memory_space=pl.ANY)
    smem = pl.BlockSpec(memory_space=pltpu.SMEM)
    out = jax.ShapeDtypeStruct(prior_weight.shape, jnp.float32)
    f32 = lambda *shape: pltpu.VMEM(shape, jnp.float32)
    b16 = lambda *shape: pltpu.VMEM(shape, jnp.bfloat16)
    return pl.pallas_call(
        functools.partial(kernel, nb, scale, period),
        out_shape=(out, out),
        in_specs=[hbm, hbm, vmem, vmem, vmem, vmem, smem],
        out_specs=(vmem, vmem),
        scratch_shapes=[
            f32(rows, width),
            f32(rows, width),
            f32(DEG, half, pairs_dev, rings),
            b16(INNER, 2 * cols),
            b16(INNER, 2 * cols),
            b16(outer * rows, INNER),
            b16(outer * rows, INNER),
            b16(outer * rows, 2 * cols),
            b16(outer * rows, 2 * cols),
            f32(INNER // FINE, cols),
            f32(INNER // FINE, cols),
            f32(FINE, cols),
            f32(FINE, cols),
            f32(outer, cols),
            f32(outer, cols),
            f32(pairs, 128),
            f32(half, pairs_dev, 128),
            f32(2, half, pairs_dev, DEG),
            f32(4, 2, half, pairs_dev, DEG),
            f32(6, nb, 8, 128),
            f32(6, 2 * nb, 8, 128),
            pltpu.SemaphoreType.DMA((2,)),
            pltpu.SemaphoreType.DMA((6,)),
            pltpu.SemaphoreType.DMA((6,)),
        ],
        compiler_params=pltpu.CompilerParams(
            collective_id=0, has_side_effects=True, vmem_limit_bytes=58 * 2**20
        ),
        name="wiener",
    )(
        sky_map, noise_weight, prior_weight, seeds, loop_cos[None, :],
        jnp.transpose(pair_m), block_count,
    )


def solution(mesh):
    placed = (
        P("blk", "rep"),
        P("blk", "rep"),
        P("blk", "rep", None, None),
        P("blk", "rep", None, None),
        P(),
        P(),
        P("blk"),
    )
    return jax.shard_map(
        shards,
        mesh=mesh,
        in_specs=placed,
        out_specs=(P("blk", "rep", None, None), P("blk", "rep", None, None)),
        check_vma=False,
    )
```

```python
import functools
import math

import jax
import jax.numpy as jnp
from jax import lax
from jax.experimental import pallas as pl
from jax.experimental.pallas import tpu as pltpu
from jax.sharding import PartitionSpec as P

DEG = 128
INNER = 1024
FINE = 32
MESH = pl.DeviceIdType.MESH


def split(x):
    hi = x.astype(jnp.bfloat16)
    return hi, (x - hi.astype(jnp.float32)).astype(jnp.bfloat16)


def kernel(
    nb, scale, period,
    sky_in, noise_in, prior_in, seeds, lcos, every_m, counts,
    sol, res,
    sky, noise, legendre, basis_hi, basis_lo, pix_hi, pix_lo, st_hi, st_lo,
    cos_a, sin_a, cos_b, sin_b, cos_o, sin_o, by_pair, side, prior,
    vecs, send, recv, gram_out, gram_in, load_sem, share_send, share_recv, send_sem, recv_sem,
):
    _, rows, width = sky.shape
    chunk = width // INNER
    outer = 2 * chunk
    cols = cos_o.shape[1]
    pairs = cols // 2
    half = side.shape[0]
    rings = lcos.shape[1]
    groups = rings // 128
    n = 2 * nb
    k = lax.axis_index("blk")
    c = lax.axis_index("rep")
    me = 2 * k + c
    chunk_rows = chunk * rows

    def peer_of(d):
        peer = lax.rem(me + d, n)
        return peer // 2, lax.rem(peer, 2)

    mine = pl.ds(pl.multiple_of(c * rows, rows), rows)
    theirs = pl.ds(pl.multiple_of((1 - c) * rows, rows), rows)
    loads, shares = [], []
    for at, (src, dst) in enumerate(((sky_in, sky), (noise_in, noise))):
        loads.append(pltpu.make_async_copy(src.at[mine, :], dst.at[c], load_sem.at[at]))
        shares.append(
            pltpu.make_async_remote_copy(
                src_ref=src.at[theirs, :],
                dst_ref=dst.at[c],
                send_sem=share_send.at[at],
                recv_sem=share_recv.at[at],
                device_id=(k, 1 - c),
                device_id_type=MESH,
            )
        )
    for load in loads:
        load.start()
    barrier = pltpu.get_barrier_semaphore()

    def greet(d, _):
        pk, pc = peer_of(d)
        pl.semaphore_signal(barrier, inc=1, device_id=(pk, pc), device_id_type=MESH)
        return 0

    lax.fori_loop(1, n, greet, 0)

    def post(src, dst, at, spread_out):
        pick = lambda pk, pc: 2 * pk + pc if spread_out else pk

        def one(d, _):
            pk, pc = peer_of(d)
            pltpu.make_async_remote_copy(
                src_ref=src.at[pick(pk, pc)],
                dst_ref=dst.at[me],
                send_sem=send_sem.at[at],
                recv_sem=recv_sem.at[at],
                device_id=(pk, pc),
                device_id_type=MESH,
            ).start()
            return 0

        lax.fori_loop(1, n, one, 0)
        dst[me] = src[pick(k, c)]

    def drain(dst, at, sem):
        block = dst.at[pl.ds(0, n - 1)]
        pltpu.make_async_copy(block, block, sem.at[at]).wait()

    m_row = jnp.concatenate([every_m[0:1, :], every_m[1:2, :]], axis=1)

    def trig(count, base, step, cos_ref, sin_ref):
        at = base + step * lax.broadcasted_iota(jnp.int32, (count, cols), 0)
        cos_ref[...], sin_ref[...] = phases(at * m_row, period)

    trig(INNER // FINE, 0, FINE, cos_a, sin_a)
    trig(FINE, 0, 1, cos_b, sin_b)
    trig(outer, 0, INNER, cos_o, sin_o)
    pl.semaphore_wait(barrier, n - 1)
    for share in shares:
        share.start()

    def make_basis(a, _):
        ca, sa = cos_a[pl.ds(a, 1), :], sin_a[pl.ds(a, 1), :]
        cb, sb = cos_b[...], sin_b[...]
        where = pl.ds(pl.multiple_of(a * FINE, FINE), FINE)
        hi, lo = split(ca * cb - sa * sb)
        basis_hi[where, :cols] = hi
        basis_lo[where, :cols] = lo
        hi, lo = split(sa * cb + ca * sb)
        basis_hi[where, cols:] = hi
        basis_lo[where, cols:] = lo
        return 0

    lax.fori_loop(0, INNER // FINE, make_basis, 0)

    def first_pixels(side_id):
        def one(j, _):
            lanes = pl.ds(pl.multiple_of(j * INNER, INNER), INNER)
            hi, lo = split(sky[side_id, :, lanes] * noise[side_id, :, lanes])
            where = pl.ds(pl.multiple_of((side_id * chunk + j) * rows, rows), rows)
            pix_hi[where, :] = hi
            pix_lo[where, :] = lo
            return 0

        lax.fori_loop(0, chunk, one, 0)

    vecs[0] = jnp.zeros(vecs.shape[1:], jnp.float32)

    row_id = lax.broadcasted_iota(jnp.int32, (8, 128), 0)
    lane = lax.broadcasted_iota(jnp.int32, (8, 128), 1)

    def make_legendre():
        m_float = every_m[...].astype(jnp.float32)
        by_pair[...] = jnp.transpose(
            jnp.concatenate([m_float, jnp.zeros((126, pairs), jnp.float32)], axis=0)
        )
        local = by_pair[pl.ds(pl.multiple_of(k * 8, 8), 8), :]
        m_first = jnp.broadcast_to(local[:, 0:1], (8, 128)).astype(jnp.int32)
        m_second = jnp.broadcast_to(local[:, 1:2], (8, 128)).astype(jnp.int32)
        count = jnp.zeros((8, 128), jnp.int32)
        for p in range(8):
            count = jnp.where(row_id == p, counts[p], count)
        coefs = []
        for b in range(half):
            block = c * half + b
            second = count <= block
            offset = jnp.where(second, block - count, block)
            column = jnp.where(second, m_second, m_first)
            degree = 128 * (lax.shift_right_logical(17 * column, 11) + 1) + 128 * offset + lane
            coefs.append((ladder(degree, column), 1.0 / ladder(degree - 1, column)))
            side[b] = jnp.where(second, 1.0, 0.0)
            for t in range(2):
                prior[t, b] = jnp.concatenate(
                    [prior_in[p, b, t:t + 1, :] for p in range(8)], axis=0
                )
        x = jnp.broadcast_to(lcos[...], (8, rings))
        wide = lambda a, u: jnp.concatenate(
            [jnp.broadcast_to(a[:, u:u + 1], (8, 128))] * groups, axis=-1
        )
        state = []
        for b in range(half):
            for i in range(2):
                state.append(
                    jnp.concatenate([seeds[p, b, i:i + 1, :] for p in range(8)], axis=0)
                )
                legendre[i, b] = state[-1]

        def advance(i, u, coefs, state):
            out = []
            for b in range(half):
                earlier, latest = state[2 * b:2 * b + 2]
                ca, cb = coefs[2 * b:2 * b + 2]
                now = wide(ca, u) * (x * latest - wide(cb, u) * earlier)
                legendre[i, b] = now
                out += [latest, now]
            return out

        coefs = [v for pair in coefs for v in pair]
        for i in range(2, 8):
            state = advance(i, i, coefs, state)

        def step(g, packed):
            coefs, state = packed
            coefs = tuple(pltpu.roll(v, 120, 1) for v in coefs)
            for u in range(8):
                state = advance(g * 8 + u, u, coefs, state)
            return coefs, tuple(state)

        lax.fori_loop(1, DEG // 8, step, (tuple(coefs), tuple(state)))

    def dots(a_hi, a_lo, b_hi, b_lo, dims):
        dot = functools.partial(
            lax.dot_general, dimension_numbers=dims, preferred_element_type=jnp.float32
        )
        both = dot(jnp.concatenate([a_hi, a_lo], axis=0), b_hi)
        size = a_hi.shape[0]
        return both[:size] + (both[size:] + dot(a_hi, b_lo))

    def forward(it):
        def half_of_loop(h, sums):
            re, im = sums
            part = lax.rem(h + c, 2)

            @pl.when(it == 0)
            def _():
                @pl.when(h == 0)
                def _():
                    for load in loads:
                        load.wait()

                @pl.when(h == 1)
                def _():
                    for share in shares:
                        share.wait_recv()

                first_pixels(part)

            where = pl.ds(pl.multiple_of(part * chunk_rows, chunk_rows), chunk_rows)
            sect = dots(
                pix_hi[where, :], pix_lo[where, :], basis_hi[...], basis_lo[...],
                (((1,), (0,)), ((), ())),
            )
            for u in range(chunk):
                co = cos_o[pl.ds(part * chunk + u, 1), :]
                so = sin_o[pl.ds(part * chunk + u, 1), :]
                cs = sect[u * rows:(u + 1) * rows, :cols]
                ss = sect[u * rows:(u + 1) * rows, cols:]
                re = re + (cs * co - ss * so)
                im = im - (ss * co + cs * so)
            return re, im

        zero = jnp.zeros((rows, cols), jnp.float32)
        re, im = lax.fori_loop(0, 2, half_of_loop, (zero, zero))
        stacked = scale * jnp.concatenate(
            [re[:, :pairs], im[:, :pairs], re[:, pairs:], im[:, pairs:]], axis=0
        )
        stacked = jnp.transpose(
            jnp.concatenate([stacked, jnp.zeros((64, pairs), jnp.float32)], axis=0)
        )
        for q in range(nb):
            pack(send.at[2 * it, q], stacked[8 * q:8 * q + 8, :64])

    def pack(ref, tile):
        ref[...] = jnp.concatenate([tile[:4], tile[4:]], axis=1)

    def unpack(tile):
        return jnp.concatenate([tile[:, :64], tile[:, 64:]], axis=0)

    def spread(phase):
        got = [unpack(recv[phase, q]) for q in range(n)]
        gathered = []
        for part in range(4):
            at = part * rows
            gathered.append(
                jnp.concatenate([g[:, at:at + rows] for g in got], axis=1)
            )
        spec = {}
        for b in range(2):
            mask = jnp.concatenate([side[b]] * groups, axis=-1) > 0.5
            for t in range(2):
                spec[t, b] = jnp.where(mask, gathered[2 + t], gathered[t])

        def step(g, acc):
            acc = list(acc)
            for u in range(8):
                i = g * 8 + u
                for b in range(2):
                    leg = legendre[i, b]
                    for t in range(2):
                        prod = leg * spec[t, b]
                        tot = prod[:, :128]
                        for q in range(1, groups):
                            tot = tot + prod[:, q * 128:(q + 1) * 128]
                        val = jnp.sum(tot, axis=1, keepdims=True)
                        acc[2 * t + b] = jnp.where(lane == i, val, acc[2 * t + b])
            return tuple(acc)

        zero = jnp.zeros((8, 128), jnp.float32)
        return lax.fori_loop(0, DEG // 8, step, (zero,) * 4)

    def gather_columns(vec, phase):
        def step(g, packed):
            coef, acc = packed
            acc = list(acc)
            for u in range(8):
                for b in range(2):
                    leg = legendre[g * 8 + u, b]
                    for t in range(2):
                        acc[2 * t + b] = acc[2 * t + b] + leg * coef[2 * t + b][:, u:u + 1]
            coef = tuple(pltpu.roll(x, 120, 1) for x in coef)
            return coef, tuple(acc)

        zero = jnp.zeros((8, rings), jnp.float32)
        _, acc = lax.fori_loop(0, DEG // 8, step, (tuple(vec), (zero,) * 4))
        parts = []
        for s in range(2):
            for t in range(2):
                tot = None
                for b in range(2):
                    mask = jnp.concatenate([side[b]] * groups, axis=-1) > 0.5
                    f = acc[2 * t + b]
                    f = jnp.where(mask, f, 0.0) if s else jnp.where(mask, 0.0, f)
                    tot = f if tot is None else tot + f
                parts.append(tot)
        for q in range(n):
            pack(send.at[phase, q], jnp.concatenate(
                [x[:, q * rows:(q + 1) * rows] for x in parts], axis=1
            ))

    def inverse(phase):
        table = jnp.concatenate(
            [unpack(recv[phase, 2 * q] + recv[phase, 2 * q + 1]) for q in range(nb)], axis=0
        )
        table = jnp.concatenate([table, jnp.zeros((pairs, 64), jnp.float32)], axis=1)
        table = scale * jnp.transpose(table)
        re = jnp.concatenate([table[:rows], table[2 * rows:3 * rows]], axis=1)
        im = jnp.concatenate([table[rows:2 * rows], table[3 * rows:4 * rows]], axis=1)

        def mix(j, _):
            co, so = cos_o[pl.ds(j, 1), :], sin_o[pl.ds(j, 1), :]
            where = pl.ds(pl.multiple_of(j * rows, rows), rows)
            hi, lo = split(re * co - im * so)
            st_hi[where, :cols] = hi
            st_lo[where, :cols] = lo
            hi, lo = split(-(re * so + im * co))
            st_hi[where, cols:] = hi
            st_lo[where, cols:] = lo
            return 0

        lax.fori_loop(0, outer, mix, 0)

        def half_of_loop(h, energy):
            where = pl.ds(pl.multiple_of(h * chunk_rows, chunk_rows), chunk_rows)
            pix = dots(
                st_hi[where, :], st_lo[where, :], basis_hi[...], basis_lo[...],
                (((1,), (1,)), ((), ())),
            )
            for u in range(chunk):
                j = h * chunk + u
                weight = noise[h, :, u * INNER:(u + 1) * INNER]
                values = pix[u * rows:(u + 1) * rows]
                weighted = weight * values
                power = weighted * values
                for q in range(INNER // 128):
                    energy = energy + power[:, q * 128:(q + 1) * 128]
                hi, lo = split(weighted)
                at = pl.ds(pl.multiple_of(j * rows, rows), rows)
                pix_hi[at, :] = hi
                pix_lo[at, :] = lo
            return energy

        return lax.fori_loop(0, 2, half_of_loop, jnp.zeros((rows, 128), jnp.float32))

    def dot_lanes(a, b):
        x = (a * b).reshape(4, 8, 128)
        return jnp.sum(x[0] + x[1] + (x[2] + x[3]), axis=0, keepdims=True)

    def post_gram():
        def one(d, _):
            pk, pc = peer_of(d)
            pltpu.make_async_remote_copy(
                src_ref=gram_out.at[0],
                dst_ref=gram_in.at[me],
                send_sem=send_sem.at[5],
                recv_sem=recv_sem.at[5],
                device_id=(pk, pc),
                device_id_type=MESH,
            ).start()
            return 0

        lax.fori_loop(1, n, one, 0)
        gram_in[me] = gram_out[0]

    def turn(it, _):
        forward(it)
        post(send.at[2 * it], recv.at[2 * it], 2 * it, False)

        @pl.when(it == 0)
        def _():
            make_legendre()

        drain(recv.at[2 * it], 2 * it, recv_sem)
        out = spread(2 * it)
        vec = []
        for t in range(2):
            for b in range(2):
                vec.append(prior[t, b] * vecs[it, t, b] + out[2 * t + b])
                vecs[it + 1, t, b] = vec[-1]

        @pl.when(it < 2)
        def _():
            gather_columns(vec, 2 * it + 1)
            post(send.at[2 * it + 1], recv.at[2 * it + 1], 2 * it + 1, True)
            drain(recv.at[2 * it + 1], 2 * it + 1, recv_sem)
            energy = inverse(2 * it + 1)

            @pl.when(it == 1)
            def _():
                v0, v1 = vecs[1], vecs[2]
                bent = dot_lanes(v1, prior[...] * v1) + jnp.sum(energy, axis=0, keepdims=True)
                gram_out[0] = jnp.concatenate(
                    [dot_lanes(v0, v0), dot_lanes(v0, v1), dot_lanes(v1, v1), bent,
                     jnp.zeros((4, 128), jnp.float32)], axis=0
                )
                post_gram()

        return 0

    lax.fori_loop(0, 3, turn, 0)

    v0, v1, v2 = vecs[1], vecs[2], vecs[3]

    drain(gram_in, 5, recv_sem)
    gram = jnp.sum(jnp.sum(gram_in[...], axis=0), axis=1, keepdims=True)
    bb, bv, vv, vw = (gram[q:q + 1] for q in range(4))
    alpha = bb / bv
    norm = bb - 2.0 * alpha * bv + alpha * alpha * vv
    beta = norm / bb
    more = 1.0 + beta
    curve = more * more * bv - 2.0 * more * alpha * vv + alpha * alpha * vw
    alpha2 = norm / curve
    for t in range(2):
        for b in range(2):
            b0, b1, b2 = v0[t, b], v1[t, b], v2[t, b]
            r1 = b0 - alpha * b1
            d1 = r1 + beta * b0
            found = alpha * b0 + alpha2 * d1
            left = r1 - alpha2 * (more * b1 - alpha * b2)
            for p in range(8):
                sol[p, b, t:t + 1, :] = found[p:p + 1]
                res[p, b, t:t + 1, :] = left[p:p + 1]

    def finish(phase, _):
        drain(recv.at[phase], phase, send_sem)
        return 0

    lax.fori_loop(0, 5, finish, 0)
    drain(gram_in, 5, send_sem)
    for share in shares:
        share.wait_send()


def ladder(degree, column_m):
    degree_f = degree.astype(jnp.float32)
    m_over_l = column_m.astype(jnp.float32) / degree_f
    return jnp.sqrt((4.0 - 1.0 / (degree_f * degree_f)) / ((1.0 - m_over_l) * (1.0 + m_over_l)))


def phases(cycles, period):
    quarter = period // 4
    if period & (period - 1) == 0:
        cycles = cycles & (period - 1)
        turn = lax.shift_right_logical(cycles + quarter // 2, quarter.bit_length() - 1)
    else:
        cycles = lax.rem(cycles, period)
        turn = lax.div(cycles + quarter // 2, quarter)
    x = (cycles - quarter * turn).astype(jnp.float32) * (2.0 * math.pi / period)
    y = x * x
    sin = x * (1 + y * (-1 / 6 + y * (1 / 120 + y * (-1 / 5040 + y * (1 / 362880)))))
    cos = 1 + y * (-1 / 2 + y * (1 / 24 + y * (-1 / 720 + y * (1 / 40320 - y * (1 / 3628800)))))
    odd = (turn & 1) == 1
    cos_abs, sin_abs = jnp.where(odd, sin, cos), jnp.where(odd, cos, sin)
    return (
        jnp.where(((turn + 1) & 2) == 2, -cos_abs, cos_abs),
        jnp.where((turn & 2) == 2, -sin_abs, sin_abs),
    )


def shards(sky_map, noise_weight, prior_weight, seeds, loop_cos, pair_m, block_count):
    nb = lax.axis_size("blk")
    pairs_dev = block_count.shape[0]
    half = seeds.shape[1]
    rings = loop_cos.shape[0]
    pairs = pair_m.shape[0]
    cols = 2 * pairs
    rows, width = sky_map.shape
    period = width * lax.axis_size("rep")
    scale = 1.0 / math.sqrt(rings * period)
    rows = rows // 2
    outer = period // INNER
    vmem = pl.BlockSpec(memory_space=pltpu.VMEM)
    hbm = pl.BlockSpec(memory_space=pl.ANY)
    smem = pl.BlockSpec(memory_space=pltpu.SMEM)
    out = jax.ShapeDtypeStruct(prior_weight.shape, jnp.float32)
    f32 = lambda *shape: pltpu.VMEM(shape, jnp.float32)
    b16 = lambda *shape: pltpu.VMEM(shape, jnp.bfloat16)
    return pl.pallas_call(
        functools.partial(kernel, nb, scale, period),
        out_shape=(out, out),
        in_specs=[hbm, hbm, vmem, vmem, vmem, vmem, smem],
        out_specs=(vmem, vmem),
        scratch_shapes=[
            f32(2, rows, width),
            f32(2, rows, width),
            f32(DEG, half, pairs_dev, rings),
            b16(INNER, 2 * cols),
            b16(INNER, 2 * cols),
            b16(outer * rows, INNER),
            b16(outer * rows, INNER),
            b16(outer * rows, 2 * cols),
            b16(outer * rows, 2 * cols),
            f32(INNER // FINE, cols),
            f32(INNER // FINE, cols),
            f32(FINE, cols),
            f32(FINE, cols),
            f32(outer, cols),
            f32(outer, cols),
            f32(pairs, 128),
            f32(half, pairs_dev, 128),
            f32(2, half, pairs_dev, DEG),
            f32(4, 2, half, pairs_dev, DEG),
            f32(5, 2 * nb, 4, 128),
            f32(5, 2 * nb, 4, 128),
            f32(1, 8, 128),
            f32(2 * nb, 8, 128),
            pltpu.SemaphoreType.DMA((2,)),
            pltpu.SemaphoreType.DMA((2,)),
            pltpu.SemaphoreType.DMA((2,)),
            pltpu.SemaphoreType.DMA((6,)),
            pltpu.SemaphoreType.DMA((6,)),
        ],
        compiler_params=pltpu.CompilerParams(
            collective_id=0, has_side_effects=True, vmem_limit_bytes=58 * 2**20
        ),
        name="wiener",
    )(
        sky_map, noise_weight, prior_weight, seeds, loop_cos[None, :],
        jnp.transpose(pair_m), block_count,
    )


def solution(mesh):
    placed = (
        P("blk", "rep"),
        P("blk", "rep"),
        P("blk", "rep", None, None),
        P("blk", "rep", None, None),
        P(),
        P(),
        P("blk"),
    )
    return jax.shard_map(
        shards,
        mesh=mesh,
        in_specs=placed,
        out_specs=(P("blk", "rep", None, None), P("blk", "rep", None, None)),
        check_vma=False,
    )
```

```python
import functools
import math

import jax
import jax.numpy as jnp
from jax import lax
from jax.experimental import pallas as pl
from jax.experimental.pallas import tpu as pltpu
from jax.sharding import PartitionSpec as P

DEG = 128
INNER = 1024
FINE = 32
CHUNK = 8
MESH = pl.DeviceIdType.MESH


def split(x):
    hi = x.astype(jnp.bfloat16)
    return hi, (x - hi.astype(jnp.float32)).astype(jnp.bfloat16)


def kernel(
    nb, scale, period,
    sky_in, noise_in, prior_in, seeds, lcos, every_m, counts,
    both,
    sky, noise, legendre, basis_hi, basis_lo, pix_hi, pix_lo, st_hi, st_lo,
    cos_a, sin_a, cos_b, sin_b, cos_o, sin_o, by_pair, side, prior,
    vecs, send, recv, load_sem, send_sem, recv_sem,
):
    rows, width = sky.shape
    outer = width // INNER
    cols = cos_o.shape[1]
    pairs = cols // 2
    half = side.shape[0]
    rings = lcos.shape[1]
    groups = rings // 128
    per = 128 // rows
    n = 2 * nb
    k = lax.axis_index("blk")
    c = lax.axis_index("rep")
    me = c * nb + k
    chunk_rows = CHUNK * rows

    unroll = 5 if (nb - 1) % 5 == 0 else 3 if (nb - 1) % 3 == 0 else 1

    def each_peer(visit):
        visit(k, 1 - c)

        def some(g, _):
            for u in range(unroll):
                pk = k + g * unroll + (u + 1)
                pk = jnp.where(pk >= nb, pk - nb, pk)
                visit(pk, c)
                visit(pk, 1 - c)
            return 0

        lax.fori_loop(0, (nb - 1) // unroll, some, 0)

    loads = [
        pltpu.make_async_copy(sky_in, sky, load_sem.at[0]),
        pltpu.make_async_copy(noise_in, noise, load_sem.at[1]),
    ]
    for load in loads:
        load.start()
    barrier = pltpu.get_barrier_semaphore()

    def greet(pk, pc):
        pl.semaphore_signal(barrier, inc=1, device_id=(pk, pc), device_id_type=MESH)

    each_peer(greet)

    def post(phase, common):
        def one(pk, pc):
            pltpu.make_async_remote_copy(
                src_ref=send.at[phase, 0 if common else pk],
                dst_ref=recv.at[phase, me],
                send_sem=send_sem.at[phase],
                recv_sem=recv_sem.at[phase],
                device_id=(pk, pc),
                device_id_type=MESH,
            ).start()

        each_peer(one)
        recv[phase, me] = send[phase, 0 if common else k]

    def drain(phase, sem):
        block = recv.at[phase, pl.ds(0, n - 1)]
        pltpu.make_async_copy(block, block, sem.at[phase]).wait()

    m_row = jnp.concatenate([every_m[0:1, :], every_m[1:2, :]], axis=1)

    def trig(count, base, step, cos_ref, sin_ref):
        at = base + step * lax.broadcasted_iota(jnp.int32, (count, cols), 0)
        cos_ref[...], sin_ref[...] = phases(at * m_row, period)

    trig(INNER // FINE, 0, FINE, cos_a, sin_a)
    trig(FINE, 0, 1, cos_b, sin_b)
    trig(outer, c * width, INNER, cos_o, sin_o)

    def make_basis(a, _):
        ca, sa = cos_a[pl.ds(a, 1), :], sin_a[pl.ds(a, 1), :]
        cb, sb = cos_b[...], sin_b[...]
        where = pl.ds(pl.multiple_of(a * FINE, FINE), FINE)
        hi, lo = split(ca * cb - sa * sb)
        basis_hi[where, :cols] = hi
        basis_lo[where, :cols] = lo
        hi, lo = split(sa * cb + ca * sb)
        basis_hi[where, cols:] = hi
        basis_lo[where, cols:] = lo
        return 0

    lax.fori_loop(0, INNER // FINE, make_basis, 0)

    for load in loads:
        load.wait()

    def first_pixels(j, _):
        lanes = pl.ds(pl.multiple_of(j * INNER, INNER), INNER)
        hi, lo = split(sky[:, lanes] * noise[:, lanes])
        where = pl.ds(pl.multiple_of(j * rows, rows), rows)
        pix_hi[where, :] = hi
        pix_lo[where, :] = lo
        return 0

    lax.fori_loop(0, outer, first_pixels, 0)
    vecs[0] = jnp.zeros(vecs.shape[1:], jnp.float32)

    row_id = lax.broadcasted_iota(jnp.int32, (8, 128), 0)
    lane = lax.broadcasted_iota(jnp.int32, (8, 128), 1)

    def make_legendre():
        m_float = every_m[...].astype(jnp.float32)
        by_pair[...] = jnp.transpose(
            jnp.concatenate([m_float, jnp.zeros((126, pairs), jnp.float32)], axis=0)
        )
        mine = by_pair[pl.ds(pl.multiple_of(k * 8, 8), 8), :]
        m_first = jnp.broadcast_to(mine[:, 0:1], (8, 128)).astype(jnp.int32)
        m_second = jnp.broadcast_to(mine[:, 1:2], (8, 128)).astype(jnp.int32)
        count = jnp.zeros((8, 128), jnp.int32)
        for p in range(8):
            count = jnp.where(row_id == p, counts[p], count)
        coefs = []
        for b in range(half):
            block = c * half + b
            second = count <= block
            offset = jnp.where(second, block - count, block)
            column = jnp.where(second, m_second, m_first)
            degree = 128 * (lax.shift_right_logical(17 * column, 11) + 1) + 128 * offset + lane
            coefs.append((ladder(degree, column), 1.0 / ladder(degree - 1, column)))
            side[b] = jnp.where(second, 1.0, 0.0)
            for t in range(2):
                prior[t, b] = jnp.concatenate(
                    [prior_in[p, b, t:t + 1, :] for p in range(8)], axis=0
                )
        x = jnp.broadcast_to(lcos[...], (8, rings))
        wide = lambda a, u: jnp.concatenate(
            [jnp.broadcast_to(a[:, u:u + 1], (8, 128))] * groups, axis=-1
        )
        state = []
        for b in range(half):
            for i in range(2):
                state.append(
                    jnp.concatenate([seeds[p, b, i:i + 1, :] for p in range(8)], axis=0)
                )
                legendre[i, b] = state[-1]

        def advance(i, u, coefs, state):
            out = []
            for b in range(half):
                earlier, latest = state[2 * b:2 * b + 2]
                ca, cb = coefs[2 * b:2 * b + 2]
                now = wide(ca, u) * (x * latest - wide(cb, u) * earlier)
                legendre[i, b] = now
                out += [latest, now]
            return out

        coefs = [v for pair in coefs for v in pair]
        for i in range(2, 8):
            state = advance(i, i, coefs, state)

        def step(g, packed):
            coefs, state = packed
            coefs = tuple(pltpu.roll(v, 120, 1) for v in coefs)
            for u in range(8):
                state = advance(g * 8 + u, u, coefs, state)
            return coefs, tuple(state)

        lax.fori_loop(1, DEG // 8, step, (tuple(coefs), tuple(state)))

    def dots(a_hi, a_lo, b_hi, b_lo, dims):
        depth = dims[0][1][0]
        return lax.dot_general(
            jnp.concatenate([a_hi, a_lo, a_hi], axis=1),
            jnp.concatenate([b_hi, b_hi, b_lo], axis=depth),
            dimension_numbers=dims,
            preferred_element_type=jnp.float32,
        )

    def forward(phase):
        def chunk(h, sums):
            re, im = sums
            where = pl.ds(pl.multiple_of(h * chunk_rows, chunk_rows), chunk_rows)
            sect = dots(
                pix_hi[where, :], pix_lo[where, :], basis_hi[...], basis_lo[...],
                (((1,), (0,)), ((), ())),
            )
            for u in range(CHUNK):
                co = cos_o[pl.ds(h * CHUNK + u, 1), :]
                so = sin_o[pl.ds(h * CHUNK + u, 1), :]
                cs = sect[u * rows:(u + 1) * rows, :cols]
                ss = sect[u * rows:(u + 1) * rows, cols:]
                re = re + (cs * co - ss * so)
                im = im - (ss * co + cs * so)
            return re, im

        zero = jnp.zeros((rows, cols), jnp.float32)
        re, im = lax.fori_loop(0, outer // CHUNK, chunk, (zero, zero))
        stacked = scale * jnp.concatenate(
            [re[:, :pairs], im[:, :pairs], re[:, pairs:], im[:, pairs:]], axis=0
        )
        send[phase] = jnp.transpose(stacked).reshape(nb, 8, 128)

    def spread(phase):
        got = [recv[phase, q] + recv[phase, nb + q] for q in range(nb)]
        gathered = []
        for part in range(4):
            at = part * rows
            gathered.append(
                jnp.concatenate([g[:, at:at + rows] for g in got], axis=1)
            )
        spec = {}
        for b in range(2):
            mask = jnp.concatenate([side[b]] * groups, axis=-1) > 0.5
            for t in range(2):
                spec[t, b] = jnp.where(mask, gathered[2 + t], gathered[t])

        def step(g, acc):
            acc = list(acc)
            for u in range(8):
                i = g * 8 + u
                for b in range(2):
                    leg = legendre[i, b]
                    for t in range(2):
                        prod = leg * spec[t, b]
                        tot = prod[:, :128]
                        for q in range(1, groups):
                            tot = tot + prod[:, q * 128:(q + 1) * 128]
                        val = jnp.sum(tot, axis=1, keepdims=True)
                        acc[2 * t + b] = jnp.where(lane == i, val, acc[2 * t + b])
            return tuple(acc)

        zero = jnp.zeros((8, 128), jnp.float32)
        return lax.fori_loop(0, DEG // 8, step, (zero,) * 4)

    def gather_columns(vec, phase):
        def step(g, packed):
            coef, acc = packed
            acc = list(acc)
            for u in range(8):
                for b in range(2):
                    leg = legendre[g * 8 + u, b]
                    for t in range(2):
                        acc[2 * t + b] = acc[2 * t + b] + leg * coef[2 * t + b][:, u:u + 1]
            coef = tuple(pltpu.roll(x, 120, 1) for x in coef)
            return coef, tuple(acc)

        zero = jnp.zeros((8, rings), jnp.float32)
        _, acc = lax.fori_loop(0, DEG // 8, step, (tuple(vec), (zero,) * 4))
        parts = []
        for s in range(2):
            for t in range(2):
                tot = None
                for b in range(2):
                    mask = jnp.concatenate([side[b]] * groups, axis=-1) > 0.5
                    f = acc[2 * t + b]
                    f = jnp.where(mask, f, 0.0) if s else jnp.where(mask, 0.0, f)
                    tot = f if tot is None else tot + f
                parts.append(tot)
        for q in range(nb):
            send[phase, q] = jnp.concatenate(
                [x[:, q * rows:(q + 1) * rows] for x in parts], axis=1
            )

    def inverse(phase):
        table = (recv[phase, pl.ds(0, nb)] + recv[phase, pl.ds(nb, nb)]).reshape(pairs, 128)
        table = scale * jnp.transpose(table)
        re = jnp.concatenate([table[:rows], table[2 * rows:3 * rows]], axis=1)
        im = jnp.concatenate([table[rows:2 * rows], table[3 * rows:]], axis=1)

        def mix(j, _):
            co, so = cos_o[pl.ds(j, 1), :], sin_o[pl.ds(j, 1), :]
            where = pl.ds(pl.multiple_of(j * rows, rows), rows)
            hi, lo = split(re * co - im * so)
            st_hi[where, :cols] = hi
            st_lo[where, :cols] = lo
            hi, lo = split(-(re * so + im * co))
            st_hi[where, cols:] = hi
            st_lo[where, cols:] = lo
            return 0

        lax.fori_loop(0, outer, mix, 0)

        def chunk(h, energy):
            where = pl.ds(pl.multiple_of(h * chunk_rows, chunk_rows), chunk_rows)
            pix = dots(
                st_hi[where, :], st_lo[where, :], basis_hi[...], basis_lo[...],
                (((1,), (1,)), ((), ())),
            )
            for u in range(CHUNK):
                j = h * CHUNK + u
                weight = noise[:, pl.ds(pl.multiple_of(j * INNER, INNER), INNER)]
                values = pix[u * rows:(u + 1) * rows]
                weighted = weight * values
                power = weighted * values
                for q in range(INNER // 128):
                    energy = energy + power[:, q * 128:(q + 1) * 128]
                hi, lo = split(weighted)
                at = pl.ds(pl.multiple_of(j * rows, rows), rows)
                pix_hi[at, :] = hi
                pix_lo[at, :] = lo
            return energy

        return lax.fori_loop(0, outer // CHUNK, chunk, jnp.zeros((rows, 128), jnp.float32))

    def dot_lanes(a, b):
        x = (a * b).reshape(4, 8, 128)
        return jnp.sum(x[0] + x[1] + (x[2] + x[3]), axis=0, keepdims=True)

    pl.semaphore_wait(barrier, n - 1)

    def turn(it, _):
        forward(2 * it)
        post(2 * it, False)

        @pl.when(it == 0)
        def _():
            make_legendre()

        drain(2 * it, recv_sem)
        out = spread(2 * it)
        vec = []
        for t in range(2):
            for b in range(2):
                vec.append(prior[t, b] * vecs[it, t, b] + out[2 * t + b])
                vecs[it + 1, t, b] = vec[-1]

        @pl.when(it < 2)
        def _():
            gather_columns(vec, 2 * it + 1)
            post(2 * it + 1, False)
            drain(2 * it + 1, recv_sem)
            energy = inverse(2 * it + 1)

            @pl.when(it == 1)
            def _():
                v0, v1 = vecs[1], vecs[2]
                bent = dot_lanes(v1, prior[...] * v1) + jnp.sum(energy, axis=0, keepdims=True)
                send[5, 0] = jnp.concatenate(
                    [dot_lanes(v0, v0), dot_lanes(v0, v1), dot_lanes(v1, v1), bent,
                     jnp.zeros((4, 128), jnp.float32)], axis=0
                )
                post(5, True)

        return 0

    lax.fori_loop(0, 3, turn, 0)

    v0, v1, v2 = vecs[1], vecs[2], vecs[3]

    drain(5, recv_sem)
    gram = jnp.sum(jnp.sum(recv[5], axis=0), axis=1, keepdims=True)
    bb, bv, vv, vw = (gram[q:q + 1] for q in range(4))
    alpha = bb / bv
    norm = bb - 2.0 * alpha * bv + alpha * alpha * vv
    beta = norm / bb
    more = 1.0 + beta
    curve = more * more * bv - 2.0 * more * alpha * vv + alpha * alpha * vw
    alpha2 = norm / curve
    for t in range(2):
        for b in range(2):
            b0, b1, b2 = v0[t, b], v1[t, b], v2[t, b]
            r1 = b0 - alpha * b1
            d1 = r1 + beta * b0
            found = alpha * b0 + alpha2 * d1
            left = r1 - alpha2 * (more * b1 - alpha * b2)
            for p in range(8):
                both[0, p, b, t:t + 1, :] = found[p:p + 1]
                both[1, p, b, t:t + 1, :] = left[p:p + 1]

    def finish(phase, _):
        drain(phase, send_sem)
        return 0

    lax.fori_loop(0, 6, finish, 0)


def unpack_kernel(both, sol, res):
    sol[...] = both[0]
    res[...] = both[1]


def ladder(degree, column_m):
    degree_f = degree.astype(jnp.float32)
    m_over_l = column_m.astype(jnp.float32) / degree_f
    return jnp.sqrt((4.0 - 1.0 / (degree_f * degree_f)) / ((1.0 - m_over_l) * (1.0 + m_over_l)))


def phases(cycles, period):
    quarter = period // 4
    if period & (period - 1) == 0:
        cycles = cycles & (period - 1)
        turn = lax.shift_right_logical(cycles + quarter // 2, quarter.bit_length() - 1)
    else:
        cycles = lax.rem(cycles, period)
        turn = lax.div(cycles + quarter // 2, quarter)
    x = (cycles - quarter * turn).astype(jnp.float32) * (2.0 * math.pi / period)
    y = x * x
    sin = x * (1 + y * (-1 / 6 + y * (1 / 120 + y * (-1 / 5040 + y * (1 / 362880)))))
    cos = 1 + y * (-1 / 2 + y * (1 / 24 + y * (-1 / 720 + y * (1 / 40320 - y * (1 / 3628800)))))
    odd = (turn & 1) == 1
    cos_abs, sin_abs = jnp.where(odd, sin, cos), jnp.where(odd, cos, sin)
    return (
        jnp.where(((turn + 1) & 2) == 2, -cos_abs, cos_abs),
        jnp.where((turn & 2) == 2, -sin_abs, sin_abs),
    )


def shards(sky_map, noise_weight, prior_weight, seeds, loop_cos, pair_m, block_count):
    nb = lax.axis_size("blk")
    pairs_dev = block_count.shape[0]
    half = seeds.shape[1]
    rings = loop_cos.shape[0]
    pairs = pair_m.shape[0]
    cols = 2 * pairs
    rows, width = sky_map.shape
    period = width * lax.axis_size("rep")
    scale = 1.0 / math.sqrt(rings * period)
    outer = width // INNER
    vmem = pl.BlockSpec(memory_space=pltpu.VMEM)
    hbm = pl.BlockSpec(memory_space=pl.ANY)
    smem = pl.BlockSpec(memory_space=pltpu.SMEM)
    out = jax.ShapeDtypeStruct(prior_weight.shape, jnp.float32)
    f32 = lambda *shape: pltpu.VMEM(shape, jnp.float32)
    b16 = lambda *shape: pltpu.VMEM(shape, jnp.bfloat16)
    both = pl.pallas_call(
        functools.partial(kernel, nb, scale, period),
        out_shape=jax.ShapeDtypeStruct((2,) + prior_weight.shape, jnp.float32),
        in_specs=[hbm, hbm, vmem, vmem, vmem, vmem, smem],
        out_specs=vmem,
        scratch_shapes=[
            f32(rows, width),
            f32(rows, width),
            f32(DEG, half, pairs_dev, rings),
            b16(INNER, 2 * cols),
            b16(INNER, 2 * cols),
            b16(outer * rows, INNER),
            b16(outer * rows, INNER),
            b16(outer * rows, 2 * cols),
            b16(outer * rows, 2 * cols),
            f32(INNER // FINE, cols),
            f32(INNER // FINE, cols),
            f32(FINE, cols),
            f32(FINE, cols),
            f32(outer, cols),
            f32(outer, cols),
            f32(pairs, 128),
            f32(half, pairs_dev, 128),
            f32(2, half, pairs_dev, DEG),
            f32(4, 2, half, pairs_dev, DEG),
            f32(6, nb, 8, 128),
            f32(6, 2 * nb, 8, 128),
            pltpu.SemaphoreType.DMA((2,)),
            pltpu.SemaphoreType.DMA((6,)),
            pltpu.SemaphoreType.DMA((6,)),
        ],
        compiler_params=pltpu.CompilerParams(
            collective_id=0, has_side_effects=True, vmem_limit_bytes=58 * 2**20
        ),
        name="wiener",
    )(
        sky_map, noise_weight, prior_weight, seeds, loop_cos[None, :],
        jnp.transpose(pair_m), block_count,
    )
    return pl.pallas_call(
        unpack_kernel,
        out_shape=(out, out),
        in_specs=[vmem],
        out_specs=(vmem, vmem),
        name="outputs",
    )(both)


def solution(mesh):
    placed = (
        P("blk", "rep"),
        P("blk", "rep"),
        P("blk", "rep", None, None),
        P("blk", "rep", None, None),
        P(),
        P(),
        P("blk"),
    )
    return jax.shard_map(
        shards,
        mesh=mesh,
        in_specs=placed,
        out_specs=(P("blk", "rep", None, None), P("blk", "rep", None, None)),
        check_vma=False,
    )
```

```python
import functools
import math

import jax
import jax.numpy as jnp
from jax import lax
from jax.experimental import pallas as pl
from jax.experimental.pallas import tpu as pltpu
from jax.sharding import PartitionSpec as P

DEG = 128
INNER = 1024
FINE = 32
CHUNK = 8
MESH = pl.DeviceIdType.MESH


def split(x):
    hi = x.astype(jnp.bfloat16)
    return hi, (x - hi.astype(jnp.float32)).astype(jnp.bfloat16)


def kernel(
    nb, scale, period,
    sky_in, noise_in, prior_in, seeds, lcos, every_m, counts,
    both,
    sky, noise, legendre, basis_hi, basis_lo, pix_hi, pix_lo, st_hi, st_lo,
    cos_a, sin_a, cos_b, sin_b, cos_o, sin_o, by_pair, side, prior,
    vecs, send, recv, load_sem, send_sem, recv_sem,
):
    rows, width = sky.shape
    outer = width // INNER
    cols = cos_o.shape[1]
    pairs = cols // 2
    half = side.shape[0]
    rings = lcos.shape[1]
    groups = rings // 128
    batch = 32 if groups <= 4 else 8
    per = 128 // rows
    n = 2 * nb
    k = lax.axis_index("blk")
    c = lax.axis_index("rep")
    me = c * nb + k
    chunk_rows = CHUNK * rows

    unroll = 5 if (nb - 1) % 5 == 0 else 3 if (nb - 1) % 3 == 0 else 1

    def each_peer(visit):
        visit(k, 1 - c)

        def some(g, _):
            for u in range(unroll):
                pk = k + g * unroll + (u + 1)
                pk = jnp.where(pk >= nb, pk - nb, pk)
                visit(pk, c)
                visit(pk, 1 - c)
            return 0

        lax.fori_loop(0, (nb - 1) // unroll, some, 0)

    loads = [
        pltpu.make_async_copy(sky_in, sky, load_sem.at[0]),
        pltpu.make_async_copy(noise_in, noise, load_sem.at[1]),
    ]
    for load in loads:
        load.start()
    barrier = pltpu.get_barrier_semaphore()

    def greet(pk, pc):
        pl.semaphore_signal(barrier, inc=1, device_id=(pk, pc), device_id_type=MESH)

    each_peer(greet)

    def post(phase, common):
        def one(pk, pc):
            pltpu.make_async_remote_copy(
                src_ref=send.at[phase, 0 if common else pk],
                dst_ref=recv.at[phase, me],
                send_sem=send_sem.at[phase],
                recv_sem=recv_sem.at[phase],
                device_id=(pk, pc),
                device_id_type=MESH,
            ).start()

        each_peer(one)
        recv[phase, me] = send[phase, 0 if common else k]

    def drain(phase, sem):
        block = recv.at[phase, pl.ds(0, n - 1)]
        pltpu.make_async_copy(block, block, sem.at[phase]).wait()

    m_row = jnp.concatenate([every_m[0:1, :], every_m[1:2, :]], axis=1)

    def trig(count, base, step, cos_ref, sin_ref):
        at = base + step * lax.broadcasted_iota(jnp.int32, (count, cols), 0)
        cos_ref[...], sin_ref[...] = phases(at * m_row, period)

    trig(INNER // FINE, 0, FINE, cos_a, sin_a)
    trig(FINE, 0, 1, cos_b, sin_b)
    trig(outer, c * width, INNER, cos_o, sin_o)

    def make_basis(a, _):
        ca, sa = cos_a[pl.ds(a, 1), :], sin_a[pl.ds(a, 1), :]
        cb, sb = cos_b[...], sin_b[...]
        where = pl.ds(pl.multiple_of(a * FINE, FINE), FINE)
        hi, lo = split(ca * cb - sa * sb)
        basis_hi[where, :cols] = hi
        basis_lo[where, :cols] = lo
        hi, lo = split(sa * cb + ca * sb)
        basis_hi[where, cols:] = hi
        basis_lo[where, cols:] = lo
        return 0

    lax.fori_loop(0, INNER // FINE, make_basis, 0)

    for load in loads:
        load.wait()

    def first_pixels(j, _):
        lanes = pl.ds(pl.multiple_of(j * INNER, INNER), INNER)
        hi, lo = split(sky[:, lanes] * noise[:, lanes])
        where = pl.ds(pl.multiple_of(j * rows, rows), rows)
        pix_hi[where, :] = hi
        pix_lo[where, :] = lo
        return 0

    lax.fori_loop(0, outer, first_pixels, 0)
    vecs[0] = jnp.zeros(vecs.shape[1:], jnp.float32)

    row_id = lax.broadcasted_iota(jnp.int32, (8, 128), 0)
    lane = lax.broadcasted_iota(jnp.int32, (8, 128), 1)

    def make_legendre():
        m_float = every_m[...].astype(jnp.float32)
        by_pair[...] = jnp.transpose(
            jnp.concatenate([m_float, jnp.zeros((126, pairs), jnp.float32)], axis=0)
        )
        mine = by_pair[pl.ds(pl.multiple_of(k * 8, 8), 8), :]
        m_first = jnp.broadcast_to(mine[:, 0:1], (8, 128)).astype(jnp.int32)
        m_second = jnp.broadcast_to(mine[:, 1:2], (8, 128)).astype(jnp.int32)
        count = jnp.zeros((8, 128), jnp.int32)
        for p in range(8):
            count = jnp.where(row_id == p, counts[p], count)
        coefs = []
        for b in range(half):
            block = c * half + b
            second = count <= block
            offset = jnp.where(second, block - count, block)
            column = jnp.where(second, m_second, m_first)
            degree = 128 * (lax.shift_right_logical(17 * column, 11) + 1) + 128 * offset + lane
            coefs.append((ladder(degree, column), 1.0 / ladder(degree - 1, column)))
            side[b] = jnp.where(second, 1.0, 0.0)
            for t in range(2):
                prior[t, b] = jnp.concatenate(
                    [prior_in[p, b, t:t + 1, :] for p in range(8)], axis=0
                )
        x = jnp.broadcast_to(lcos[...], (8, rings))
        wide = lambda a, u: jnp.concatenate(
            [jnp.broadcast_to(a[:, u:u + 1], (8, 128))] * groups, axis=-1
        )
        state = []
        for b in range(half):
            for i in range(2):
                state.append(
                    jnp.concatenate([seeds[p, b, i:i + 1, :] for p in range(8)], axis=0)
                )
                legendre[i, b] = state[-1]

        def advance(i, u, coefs, state):
            out = []
            for b in range(half):
                earlier, latest = state[2 * b:2 * b + 2]
                ca, cb = coefs[2 * b:2 * b + 2]
                now = wide(ca, u) * (x * latest - wide(cb, u) * earlier)
                legendre[i, b] = now
                out += [latest, now]
            return out

        coefs = [v for pair in coefs for v in pair]
        for i in range(2, batch):
            state = advance(i, i, coefs, state)

        def step(g, packed):
            coefs, state = packed
            coefs = tuple(pltpu.roll(v, 128 - batch, 1) for v in coefs)
            for u in range(batch):
                state = advance(g * batch + u, u, coefs, state)
            return coefs, tuple(state)

        lax.fori_loop(1, DEG // batch, step, (tuple(coefs), tuple(state)))

    def dots(a_hi, a_lo, b_hi, b_lo, dims):
        depth = dims[0][1][0]
        return lax.dot_general(
            jnp.concatenate([a_hi, a_lo, a_hi], axis=1),
            jnp.concatenate([b_hi, b_hi, b_lo], axis=depth),
            dimension_numbers=dims,
            preferred_element_type=jnp.float32,
        )

    def forward(phase):
        def chunk(h, sums):
            re, im = sums
            where = pl.ds(pl.multiple_of(h * chunk_rows, chunk_rows), chunk_rows)
            sect = dots(
                pix_hi[where, :], pix_lo[where, :], basis_hi[...], basis_lo[...],
                (((1,), (0,)), ((), ())),
            )
            for u in range(CHUNK):
                co = cos_o[pl.ds(h * CHUNK + u, 1), :]
                so = sin_o[pl.ds(h * CHUNK + u, 1), :]
                cs = sect[u * rows:(u + 1) * rows, :cols]
                ss = sect[u * rows:(u + 1) * rows, cols:]
                re = re + (cs * co - ss * so)
                im = im - (ss * co + cs * so)
            return re, im

        zero = jnp.zeros((rows, cols), jnp.float32)
        re, im = lax.fori_loop(0, outer // CHUNK, chunk, (zero, zero))
        stacked = scale * jnp.concatenate(
            [re[:, :pairs], im[:, :pairs], re[:, pairs:], im[:, pairs:]], axis=0
        )
        send[phase] = jnp.transpose(stacked).reshape(nb, 8, 128)

    def spread(phase):
        got = [recv[phase, q] + recv[phase, nb + q] for q in range(nb)]
        gathered = []
        for part in range(4):
            at = part * rows
            gathered.append(
                jnp.concatenate([g[:, at:at + rows] for g in got], axis=1)
            )
        spec = {}
        for b in range(2):
            mask = jnp.concatenate([side[b]] * groups, axis=-1) > 0.5
            for t in range(2):
                spec[t, b] = jnp.where(mask, gathered[2 + t], gathered[t])

        def step(g, acc):
            acc = list(acc)
            for u in range(batch):
                i = g * batch + u
                for b in range(2):
                    leg = legendre[i, b]
                    for t in range(2):
                        prod = leg * spec[t, b]
                        tot = prod[:, :128]
                        for q in range(1, groups):
                            tot = tot + prod[:, q * 128:(q + 1) * 128]
                        val = jnp.sum(tot, axis=1, keepdims=True)
                        acc[2 * t + b] = jnp.where(lane == i, val, acc[2 * t + b])
            return tuple(acc)

        zero = jnp.zeros((8, 128), jnp.float32)
        return lax.fori_loop(0, DEG // batch, step, (zero,) * 4)

    def gather_columns(vec, phase):
        def step(g, packed):
            coef, acc = packed
            acc = list(acc)
            for u in range(batch):
                for b in range(2):
                    leg = legendre[g * batch + u, b]
                    for t in range(2):
                        acc[2 * t + b] = acc[2 * t + b] + leg * coef[2 * t + b][:, u:u + 1]
            coef = tuple(pltpu.roll(x, 128 - batch, 1) for x in coef)
            return coef, tuple(acc)

        zero = jnp.zeros((8, rings), jnp.float32)
        _, acc = lax.fori_loop(0, DEG // batch, step, (tuple(vec), (zero,) * 4))
        parts = []
        for s in range(2):
            for t in range(2):
                tot = None
                for b in range(2):
                    mask = jnp.concatenate([side[b]] * groups, axis=-1) > 0.5
                    f = acc[2 * t + b]
                    f = jnp.where(mask, f, 0.0) if s else jnp.where(mask, 0.0, f)
                    tot = f if tot is None else tot + f
                parts.append(tot)
        for q in range(nb):
            send[phase, q] = jnp.concatenate(
                [x[:, q * rows:(q + 1) * rows] for x in parts], axis=1
            )

    def inverse(phase):
        table = (recv[phase, pl.ds(0, nb)] + recv[phase, pl.ds(nb, nb)]).reshape(pairs, 128)
        table = scale * jnp.transpose(table)
        re = jnp.concatenate([table[:rows], table[2 * rows:3 * rows]], axis=1)
        im = jnp.concatenate([table[rows:2 * rows], table[3 * rows:]], axis=1)

        def mix(j, _):
            co, so = cos_o[pl.ds(j, 1), :], sin_o[pl.ds(j, 1), :]
            where = pl.ds(pl.multiple_of(j * rows, rows), rows)
            hi, lo = split(re * co - im * so)
            st_hi[where, :cols] = hi
            st_lo[where, :cols] = lo
            hi, lo = split(-(re * so + im * co))
            st_hi[where, cols:] = hi
            st_lo[where, cols:] = lo
            return 0

        lax.fori_loop(0, outer, mix, 0)

        def chunk(h, energy):
            where = pl.ds(pl.multiple_of(h * chunk_rows, chunk_rows), chunk_rows)
            pix = dots(
                st_hi[where, :], st_lo[where, :], basis_hi[...], basis_lo[...],
                (((1,), (1,)), ((), ())),
            )
            for u in range(CHUNK):
                j = h * CHUNK + u
                weight = noise[:, pl.ds(pl.multiple_of(j * INNER, INNER), INNER)]
                values = pix[u * rows:(u + 1) * rows]
                weighted = weight * values
                power = weighted * values
                for q in range(INNER // 128):
                    energy = energy + power[:, q * 128:(q + 1) * 128]
                hi, lo = split(weighted)
                at = pl.ds(pl.multiple_of(j * rows, rows), rows)
                pix_hi[at, :] = hi
                pix_lo[at, :] = lo
            return energy

        return lax.fori_loop(0, outer // CHUNK, chunk, jnp.zeros((rows, 128), jnp.float32))

    def dot_lanes(a, b):
        x = (a * b).reshape(4, 8, 128)
        return jnp.sum(x[0] + x[1] + (x[2] + x[3]), axis=0, keepdims=True)

    pl.semaphore_wait(barrier, n - 1)

    def turn(it, _):
        forward(2 * it)
        post(2 * it, False)

        @pl.when(it == 0)
        def _():
            make_legendre()

        drain(2 * it, recv_sem)
        out = spread(2 * it)
        vec = []
        for t in range(2):
            for b in range(2):
                vec.append(prior[t, b] * vecs[it, t, b] + out[2 * t + b])
                vecs[it + 1, t, b] = vec[-1]

        @pl.when(it < 2)
        def _():
            gather_columns(vec, 2 * it + 1)
            post(2 * it + 1, False)
            drain(2 * it + 1, recv_sem)
            energy = inverse(2 * it + 1)

            @pl.when(it == 1)
            def _():
                v0, v1 = vecs[1], vecs[2]
                bent = dot_lanes(v1, prior[...] * v1) + jnp.sum(energy, axis=0, keepdims=True)
                send[5, 0] = jnp.concatenate(
                    [dot_lanes(v0, v0), dot_lanes(v0, v1), dot_lanes(v1, v1), bent,
                     jnp.zeros((4, 128), jnp.float32)], axis=0
                )
                post(5, True)

        return 0

    lax.fori_loop(0, 3, turn, 0)

    v0, v1, v2 = vecs[1], vecs[2], vecs[3]

    drain(5, recv_sem)
    gram = jnp.sum(jnp.sum(recv[5], axis=0), axis=1, keepdims=True)
    bb, bv, vv, vw = (gram[q:q + 1] for q in range(4))
    alpha = bb / bv
    norm = bb - 2.0 * alpha * bv + alpha * alpha * vv
    beta = norm / bb
    more = 1.0 + beta
    curve = more * more * bv - 2.0 * more * alpha * vv + alpha * alpha * vw
    alpha2 = norm / curve
    for t in range(2):
        for b in range(2):
            b0, b1, b2 = v0[t, b], v1[t, b], v2[t, b]
            r1 = b0 - alpha * b1
            d1 = r1 + beta * b0
            found = alpha * b0 + alpha2 * d1
            left = r1 - alpha2 * (more * b1 - alpha * b2)
            for p in range(8):
                both[0, p, b, t:t + 1, :] = found[p:p + 1]
                both[1, p, b, t:t + 1, :] = left[p:p + 1]

    def finish(phase, _):
        drain(phase, send_sem)
        return 0

    lax.fori_loop(0, 6, finish, 0)


def unpack_kernel(both, sol, res):
    sol[...] = both[0]
    res[...] = both[1]


def ladder(degree, column_m):
    degree_f = degree.astype(jnp.float32)
    m_over_l = column_m.astype(jnp.float32) / degree_f
    return jnp.sqrt((4.0 - 1.0 / (degree_f * degree_f)) / ((1.0 - m_over_l) * (1.0 + m_over_l)))


def phases(cycles, period):
    quarter = period // 4
    if period & (period - 1) == 0:
        cycles = cycles & (period - 1)
        turn = lax.shift_right_logical(cycles + quarter // 2, quarter.bit_length() - 1)
    else:
        cycles = lax.rem(cycles, period)
        turn = lax.div(cycles + quarter // 2, quarter)
    x = (cycles - quarter * turn).astype(jnp.float32) * (2.0 * math.pi / period)
    y = x * x
    sin = x * (1 + y * (-1 / 6 + y * (1 / 120 + y * (-1 / 5040 + y * (1 / 362880)))))
    cos = 1 + y * (-1 / 2 + y * (1 / 24 + y * (-1 / 720 + y * (1 / 40320 - y * (1 / 3628800)))))
    odd = (turn & 1) == 1
    cos_abs, sin_abs = jnp.where(odd, sin, cos), jnp.where(odd, cos, sin)
    return (
        jnp.where(((turn + 1) & 2) == 2, -cos_abs, cos_abs),
        jnp.where((turn & 2) == 2, -sin_abs, sin_abs),
    )


def shards(sky_map, noise_weight, prior_weight, seeds, loop_cos, pair_m, block_count):
    nb = lax.axis_size("blk")
    pairs_dev = block_count.shape[0]
    half = seeds.shape[1]
    rings = loop_cos.shape[0]
    pairs = pair_m.shape[0]
    cols = 2 * pairs
    rows, width = sky_map.shape
    period = width * lax.axis_size("rep")
    scale = 1.0 / math.sqrt(rings * period)
    outer = width // INNER
    vmem = pl.BlockSpec(memory_space=pltpu.VMEM)
    hbm = pl.BlockSpec(memory_space=pl.ANY)
    smem = pl.BlockSpec(memory_space=pltpu.SMEM)
    out = jax.ShapeDtypeStruct(prior_weight.shape, jnp.float32)
    f32 = lambda *shape: pltpu.VMEM(shape, jnp.float32)
    b16 = lambda *shape: pltpu.VMEM(shape, jnp.bfloat16)
    both = pl.pallas_call(
        functools.partial(kernel, nb, scale, period),
        out_shape=jax.ShapeDtypeStruct((2,) + prior_weight.shape, jnp.float32),
        in_specs=[hbm, hbm, vmem, vmem, vmem, vmem, smem],
        out_specs=vmem,
        scratch_shapes=[
            f32(rows, width),
            f32(rows, width),
            f32(DEG, half, pairs_dev, rings),
            b16(INNER, 2 * cols),
            b16(INNER, 2 * cols),
            b16(outer * rows, INNER),
            b16(outer * rows, INNER),
            b16(outer * rows, 2 * cols),
            b16(outer * rows, 2 * cols),
            f32(INNER // FINE, cols),
            f32(INNER // FINE, cols),
            f32(FINE, cols),
            f32(FINE, cols),
            f32(outer, cols),
            f32(outer, cols),
            f32(pairs, 128),
            f32(half, pairs_dev, 128),
            f32(2, half, pairs_dev, DEG),
            f32(4, 2, half, pairs_dev, DEG),
            f32(6, nb, 8, 128),
            f32(6, 2 * nb, 8, 128),
            pltpu.SemaphoreType.DMA((2,)),
            pltpu.SemaphoreType.DMA((6,)),
            pltpu.SemaphoreType.DMA((6,)),
        ],
        compiler_params=pltpu.CompilerParams(
            collective_id=0, has_side_effects=True, vmem_limit_bytes=58 * 2**20
        ),
        name="wiener",
    )(
        sky_map, noise_weight, prior_weight, seeds, loop_cos[None, :],
        jnp.transpose(pair_m), block_count,
    )
    return pl.pallas_call(
        unpack_kernel,
        out_shape=(out, out),
        in_specs=[vmem],
        out_specs=(vmem, vmem),
        name="outputs",
    )(both)


def solution(mesh):
    placed = (
        P("blk", "rep"),
        P("blk", "rep"),
        P("blk", "rep", None, None),
        P("blk", "rep", None, None),
        P(),
        P(),
        P("blk"),
    )
    return jax.shard_map(
        shards,
        mesh=mesh,
        in_specs=placed,
        out_specs=(P("blk", "rep", None, None), P("blk", "rep", None, None)),
        check_vma=False,
    )
```

```python
import functools
import math

import jax
import jax.numpy as jnp
from jax import lax
from jax.experimental import pallas as pl
from jax.experimental.pallas import tpu as pltpu
from jax.sharding import PartitionSpec as P

DEG = 128
INNER = 1024
FINE = 32
CHUNK = 8
MESH = pl.DeviceIdType.MESH


def split(x):
    hi = x.astype(jnp.bfloat16)
    return hi, (x - hi.astype(jnp.float32)).astype(jnp.bfloat16)


def kernel(
    nb, scale, period,
    sky_in, noise_in, prior_in, seeds, lcos, every_m, counts,
    both,
    sky, noise, legendre, basis_hi, basis_lo, pix_hi, pix_lo, st_hi, st_lo,
    cos_a, sin_a, cos_b, sin_b, cos_o, sin_o, by_pair, side, prior,
    vecs, send, recv, load_sem, send_sem, recv_sem,
):
    rows, width = sky.shape
    outer = width // INNER
    cols = cos_o.shape[1]
    pairs = cols // 2
    half = side.shape[0]
    rings = lcos.shape[1]
    groups = rings // 128
    batch = 64 if groups <= 4 else 8
    per = 128 // rows
    n = 2 * nb
    k = lax.axis_index("blk")
    c = lax.axis_index("rep")
    me = c * nb + k
    chunk_rows = CHUNK * rows

    unroll = 5 if (nb - 1) % 5 == 0 else 3 if (nb - 1) % 3 == 0 else 1

    def each_peer(visit):
        visit(k, 1 - c)

        def some(g, _):
            for u in range(unroll):
                pk = k + g * unroll + (u + 1)
                pk = jnp.where(pk >= nb, pk - nb, pk)
                visit(pk, c)
                visit(pk, 1 - c)
            return 0

        lax.fori_loop(0, (nb - 1) // unroll, some, 0)

    loads = [
        pltpu.make_async_copy(sky_in, sky, load_sem.at[0]),
        pltpu.make_async_copy(noise_in, noise, load_sem.at[1]),
    ]
    for load in loads:
        load.start()
    barrier = pltpu.get_barrier_semaphore()

    def in_fours(count, visit):
        def four(g, _):
            for u in range(4):
                visit(g * 4 + u)
            return 0

        lax.fori_loop(0, count // 4, four, 0)

    def greet(pk, pc):
        pl.semaphore_signal(barrier, inc=1, device_id=(pk, pc), device_id_type=MESH)

    each_peer(greet)

    def post(phase, common):
        def one(pk, pc):
            pltpu.make_async_remote_copy(
                src_ref=send.at[phase, 0 if common else pk],
                dst_ref=recv.at[phase, me],
                send_sem=send_sem.at[phase],
                recv_sem=recv_sem.at[phase],
                device_id=(pk, pc),
                device_id_type=MESH,
            ).start()

        each_peer(one)
        recv[phase, me] = send[phase, 0 if common else k]

    def drain(phase, sem):
        block = recv.at[phase, pl.ds(0, n - 1)]
        pltpu.make_async_copy(block, block, sem.at[phase]).wait()

    m_row = jnp.concatenate([every_m[0:1, :], every_m[1:2, :]], axis=1)

    def trig(count, base, step, cos_ref, sin_ref):
        at = base + step * lax.broadcasted_iota(jnp.int32, (count, cols), 0)
        cos_ref[...], sin_ref[...] = phases(at * m_row, period)

    trig(INNER // FINE, 0, FINE, cos_a, sin_a)
    trig(FINE, 0, 1, cos_b, sin_b)
    trig(outer, c * width, INNER, cos_o, sin_o)

    def make_basis(a):
        ca, sa = cos_a[pl.ds(a, 1), :], sin_a[pl.ds(a, 1), :]
        cb, sb = cos_b[...], sin_b[...]
        where = pl.ds(pl.multiple_of(a * FINE, FINE), FINE)
        hi, lo = split(ca * cb - sa * sb)
        basis_hi[where, :cols] = hi
        basis_lo[where, :cols] = lo
        hi, lo = split(sa * cb + ca * sb)
        basis_hi[where, cols:] = hi
        basis_lo[where, cols:] = lo

    in_fours(INNER // FINE, make_basis)

    for load in loads:
        load.wait()

    def first_pixels(j, _):
        lanes = pl.ds(pl.multiple_of(j * INNER, INNER), INNER)
        hi, lo = split(sky[:, lanes] * noise[:, lanes])
        where = pl.ds(pl.multiple_of(j * rows, rows), rows)
        pix_hi[where, :] = hi
        pix_lo[where, :] = lo
        return 0

    lax.fori_loop(0, outer, first_pixels, 0)
    vecs[0] = jnp.zeros(vecs.shape[1:], jnp.float32)

    row_id = lax.broadcasted_iota(jnp.int32, (8, 128), 0)
    lane = lax.broadcasted_iota(jnp.int32, (8, 128), 1)

    def make_legendre():
        m_float = every_m[...].astype(jnp.float32)
        by_pair[...] = jnp.transpose(
            jnp.concatenate([m_float, jnp.zeros((126, pairs), jnp.float32)], axis=0)
        )
        mine = by_pair[pl.ds(pl.multiple_of(k * 8, 8), 8), :]
        m_first = jnp.broadcast_to(mine[:, 0:1], (8, 128)).astype(jnp.int32)
        m_second = jnp.broadcast_to(mine[:, 1:2], (8, 128)).astype(jnp.int32)
        count = jnp.zeros((8, 128), jnp.int32)
        for p in range(8):
            count = jnp.where(row_id == p, counts[p], count)
        coefs = []
        for b in range(half):
            block = c * half + b
            second = count <= block
            offset = jnp.where(second, block - count, block)
            column = jnp.where(second, m_second, m_first)
            degree = 128 * (lax.shift_right_logical(17 * column, 11) + 1) + 128 * offset + lane
            coefs.append((ladder(degree, column), 1.0 / ladder(degree - 1, column)))
            side[b] = jnp.where(second, 1.0, 0.0)
            for t in range(2):
                prior[t, b] = jnp.concatenate(
                    [prior_in[p, b, t:t + 1, :] for p in range(8)], axis=0
                )
        x = jnp.broadcast_to(lcos[...], (8, rings))
        wide = lambda a, u: jnp.concatenate(
            [jnp.broadcast_to(a[:, u:u + 1], (8, 128))] * groups, axis=-1
        )
        state = []
        for b in range(half):
            for i in range(2):
                state.append(
                    jnp.concatenate([seeds[p, b, i:i + 1, :] for p in range(8)], axis=0)
                )
                legendre[i, b] = state[-1]

        def advance(i, u, coefs, state):
            out = []
            for b in range(half):
                earlier, latest = state[2 * b:2 * b + 2]
                ca, cb = coefs[2 * b:2 * b + 2]
                now = wide(ca, u) * (x * latest - wide(cb, u) * earlier)
                legendre[i, b] = now
                out += [latest, now]
            return out

        coefs = [v for pair in coefs for v in pair]
        for i in range(2, batch):
            state = advance(i, i, coefs, state)

        def step(g, packed):
            coefs, state = packed
            coefs = tuple(pltpu.roll(v, 128 - batch, 1) for v in coefs)
            for u in range(batch):
                state = advance(g * batch + u, u, coefs, state)
            return coefs, tuple(state)

        lax.fori_loop(1, DEG // batch, step, (tuple(coefs), tuple(state)))

    def dots(a_hi, a_lo, b_hi, b_lo, dims):
        depth = dims[0][1][0]
        return lax.dot_general(
            jnp.concatenate([a_hi, a_lo, a_hi], axis=1),
            jnp.concatenate([b_hi, b_hi, b_lo], axis=depth),
            dimension_numbers=dims,
            preferred_element_type=jnp.float32,
        )

    def forward(phase):
        def chunk(h, sums):
            re, im = sums
            where = pl.ds(pl.multiple_of(h * chunk_rows, chunk_rows), chunk_rows)
            sect = dots(
                pix_hi[where, :], pix_lo[where, :], basis_hi[...], basis_lo[...],
                (((1,), (0,)), ((), ())),
            )
            for u in range(CHUNK):
                co = cos_o[pl.ds(h * CHUNK + u, 1), :]
                so = sin_o[pl.ds(h * CHUNK + u, 1), :]
                cs = sect[u * rows:(u + 1) * rows, :cols]
                ss = sect[u * rows:(u + 1) * rows, cols:]
                re = re + (cs * co - ss * so)
                im = im - (ss * co + cs * so)
            return re, im

        zero = jnp.zeros((rows, cols), jnp.float32)
        re, im = lax.fori_loop(0, outer // CHUNK, chunk, (zero, zero))
        stacked = scale * jnp.concatenate(
            [re[:, :pairs], im[:, :pairs], re[:, pairs:], im[:, pairs:]], axis=0
        )
        send[phase] = jnp.transpose(stacked).reshape(nb, 8, 128)

    def spread(phase):
        got = [recv[phase, q] + recv[phase, nb + q] for q in range(nb)]
        gathered = []
        for part in range(4):
            at = part * rows
            gathered.append(
                jnp.concatenate([g[:, at:at + rows] for g in got], axis=1)
            )
        spec = {}
        for b in range(2):
            mask = jnp.concatenate([side[b]] * groups, axis=-1) > 0.5
            for t in range(2):
                spec[t, b] = jnp.where(mask, gathered[2 + t], gathered[t])

        def step(g, acc):
            acc = list(acc)
            for u in range(batch):
                i = g * batch + u
                for b in range(2):
                    leg = legendre[i, b]
                    for t in range(2):
                        prod = leg * spec[t, b]
                        tot = prod[:, :128]
                        for q in range(1, groups):
                            tot = tot + prod[:, q * 128:(q + 1) * 128]
                        val = jnp.sum(tot, axis=1, keepdims=True)
                        acc[2 * t + b] = jnp.where(lane == i, val, acc[2 * t + b])
            return tuple(acc)

        zero = jnp.zeros((8, 128), jnp.float32)
        return lax.fori_loop(0, DEG // batch, step, (zero,) * 4)

    def gather_columns(vec, phase):
        def step(g, packed):
            coef, acc = packed
            acc = list(acc)
            for u in range(batch):
                for b in range(2):
                    leg = legendre[g * batch + u, b]
                    for t in range(2):
                        acc[2 * t + b] = acc[2 * t + b] + leg * coef[2 * t + b][:, u:u + 1]
            coef = tuple(pltpu.roll(x, 128 - batch, 1) for x in coef)
            return coef, tuple(acc)

        zero = jnp.zeros((8, rings), jnp.float32)
        _, acc = lax.fori_loop(0, DEG // batch, step, (tuple(vec), (zero,) * 4))
        parts = []
        for s in range(2):
            for t in range(2):
                tot = None
                for b in range(2):
                    mask = jnp.concatenate([side[b]] * groups, axis=-1) > 0.5
                    f = acc[2 * t + b]
                    f = jnp.where(mask, f, 0.0) if s else jnp.where(mask, 0.0, f)
                    tot = f if tot is None else tot + f
                parts.append(tot)
        for q in range(nb):
            send[phase, q] = jnp.concatenate(
                [x[:, q * rows:(q + 1) * rows] for x in parts], axis=1
            )

    def inverse(phase):
        table = (recv[phase, pl.ds(0, nb)] + recv[phase, pl.ds(nb, nb)]).reshape(pairs, 128)
        table = scale * jnp.transpose(table)
        re = jnp.concatenate([table[:rows], table[2 * rows:3 * rows]], axis=1)
        im = jnp.concatenate([table[rows:2 * rows], table[3 * rows:]], axis=1)

        def mix(j):
            co, so = cos_o[pl.ds(j, 1), :], sin_o[pl.ds(j, 1), :]
            where = pl.ds(pl.multiple_of(j * rows, rows), rows)
            hi, lo = split(re * co - im * so)
            st_hi[where, :cols] = hi
            st_lo[where, :cols] = lo
            hi, lo = split(-(re * so + im * co))
            st_hi[where, cols:] = hi
            st_lo[where, cols:] = lo

        in_fours(outer, mix)

        def chunk(h, energy):
            where = pl.ds(pl.multiple_of(h * chunk_rows, chunk_rows), chunk_rows)
            pix = dots(
                st_hi[where, :], st_lo[where, :], basis_hi[...], basis_lo[...],
                (((1,), (1,)), ((), ())),
            )
            for u in range(CHUNK):
                j = h * CHUNK + u
                weight = noise[:, pl.ds(pl.multiple_of(j * INNER, INNER), INNER)]
                values = pix[u * rows:(u + 1) * rows]
                weighted = weight * values
                power = weighted * values
                for q in range(INNER // 128):
                    energy = energy + power[:, q * 128:(q + 1) * 128]
                hi, lo = split(weighted)
                at = pl.ds(pl.multiple_of(j * rows, rows), rows)
                pix_hi[at, :] = hi
                pix_lo[at, :] = lo
            return energy

        return lax.fori_loop(0, outer // CHUNK, chunk, jnp.zeros((rows, 128), jnp.float32))

    def dot_lanes(a, b):
        x = (a * b).reshape(4, 8, 128)
        return jnp.sum(x[0] + x[1] + (x[2] + x[3]), axis=0, keepdims=True)

    pl.semaphore_wait(barrier, n - 1)

    def turn(it, _):
        forward(2 * it)
        post(2 * it, False)

        @pl.when(it == 0)
        def _():
            make_legendre()

        drain(2 * it, recv_sem)
        out = spread(2 * it)
        vec = []
        for t in range(2):
            for b in range(2):
                vec.append(prior[t, b] * vecs[it, t, b] + out[2 * t + b])
                vecs[it + 1, t, b] = vec[-1]

        @pl.when(it < 2)
        def _():
            gather_columns(vec, 2 * it + 1)
            post(2 * it + 1, False)
            drain(2 * it + 1, recv_sem)
            energy = inverse(2 * it + 1)

            @pl.when(it == 1)
            def _():
                v0, v1 = vecs[1], vecs[2]
                bent = dot_lanes(v1, prior[...] * v1) + jnp.sum(energy, axis=0, keepdims=True)
                send[5, 0] = jnp.concatenate(
                    [dot_lanes(v0, v0), dot_lanes(v0, v1), dot_lanes(v1, v1), bent,
                     jnp.zeros((4, 128), jnp.float32)], axis=0
                )
                post(5, True)

        return 0

    lax.fori_loop(0, 3, turn, 0)

    v0, v1, v2 = vecs[1], vecs[2], vecs[3]

    drain(5, recv_sem)
    gram = jnp.sum(jnp.sum(recv[5], axis=0), axis=1, keepdims=True)
    bb, bv, vv, vw = (gram[q:q + 1] for q in range(4))
    alpha = bb / bv
    norm = bb - 2.0 * alpha * bv + alpha * alpha * vv
    beta = norm / bb
    more = 1.0 + beta
    curve = more * more * bv - 2.0 * more * alpha * vv + alpha * alpha * vw
    alpha2 = norm / curve
    for t in range(2):
        for b in range(2):
            b0, b1, b2 = v0[t, b], v1[t, b], v2[t, b]
            r1 = b0 - alpha * b1
            d1 = r1 + beta * b0
            found = alpha * b0 + alpha2 * d1
            left = r1 - alpha2 * (more * b1 - alpha * b2)
            for p in range(8):
                both[0, p, b, t:t + 1, :] = found[p:p + 1]
                both[1, p, b, t:t + 1, :] = left[p:p + 1]

    def finish(phase, _):
        drain(phase, send_sem)
        return 0

    lax.fori_loop(0, 6, finish, 0)


def unpack_kernel(both, sol, res):
    sol[...] = both[0]
    res[...] = both[1]


def ladder(degree, column_m):
    degree_f = degree.astype(jnp.float32)
    m_over_l = column_m.astype(jnp.float32) / degree_f
    return jnp.sqrt((4.0 - 1.0 / (degree_f * degree_f)) / ((1.0 - m_over_l) * (1.0 + m_over_l)))


def phases(cycles, period):
    quarter = period // 4
    if period & (period - 1) == 0:
        cycles = cycles & (period - 1)
        turn = lax.shift_right_logical(cycles + quarter // 2, quarter.bit_length() - 1)
    else:
        cycles = lax.rem(cycles, period)
        turn = lax.div(cycles + quarter // 2, quarter)
    x = (cycles - quarter * turn).astype(jnp.float32) * (2.0 * math.pi / period)
    y = x * x
    sin = x * (1 + y * (-1 / 6 + y * (1 / 120 + y * (-1 / 5040 + y * (1 / 362880)))))
    cos = 1 + y * (-1 / 2 + y * (1 / 24 + y * (-1 / 720 + y * (1 / 40320 - y * (1 / 3628800)))))
    odd = (turn & 1) == 1
    cos_abs, sin_abs = jnp.where(odd, sin, cos), jnp.where(odd, cos, sin)
    return (
        jnp.where(((turn + 1) & 2) == 2, -cos_abs, cos_abs),
        jnp.where((turn & 2) == 2, -sin_abs, sin_abs),
    )


def shards(sky_map, noise_weight, prior_weight, seeds, loop_cos, pair_m, block_count):
    nb = lax.axis_size("blk")
    pairs_dev = block_count.shape[0]
    half = seeds.shape[1]
    rings = loop_cos.shape[0]
    pairs = pair_m.shape[0]
    cols = 2 * pairs
    rows, width = sky_map.shape
    period = width * lax.axis_size("rep")
    scale = 1.0 / math.sqrt(rings * period)
    outer = width // INNER
    vmem = pl.BlockSpec(memory_space=pltpu.VMEM)
    hbm = pl.BlockSpec(memory_space=pl.ANY)
    smem = pl.BlockSpec(memory_space=pltpu.SMEM)
    out = jax.ShapeDtypeStruct(prior_weight.shape, jnp.float32)
    f32 = lambda *shape: pltpu.VMEM(shape, jnp.float32)
    b16 = lambda *shape: pltpu.VMEM(shape, jnp.bfloat16)
    both = pl.pallas_call(
        functools.partial(kernel, nb, scale, period),
        out_shape=jax.ShapeDtypeStruct((2,) + prior_weight.shape, jnp.float32),
        in_specs=[hbm, hbm, vmem, vmem, vmem, vmem, smem],
        out_specs=vmem,
        scratch_shapes=[
            f32(rows, width),
            f32(rows, width),
            f32(DEG, half, pairs_dev, rings),
            b16(INNER, 2 * cols),
            b16(INNER, 2 * cols),
            b16(outer * rows, INNER),
            b16(outer * rows, INNER),
            b16(outer * rows, 2 * cols),
            b16(outer * rows, 2 * cols),
            f32(INNER // FINE, cols),
            f32(INNER // FINE, cols),
            f32(FINE, cols),
            f32(FINE, cols),
            f32(outer, cols),
            f32(outer, cols),
            f32(pairs, 128),
            f32(half, pairs_dev, 128),
            f32(2, half, pairs_dev, DEG),
            f32(4, 2, half, pairs_dev, DEG),
            f32(6, nb, 8, 128),
            f32(6, 2 * nb, 8, 128),
            pltpu.SemaphoreType.DMA((2,)),
            pltpu.SemaphoreType.DMA((6,)),
            pltpu.SemaphoreType.DMA((6,)),
        ],
        compiler_params=pltpu.CompilerParams(
            collective_id=0, has_side_effects=True, vmem_limit_bytes=58 * 2**20
        ),
        name="wiener",
    )(
        sky_map, noise_weight, prior_weight, seeds, loop_cos[None, :],
        jnp.transpose(pair_m), block_count,
    )
    return pl.pallas_call(
        unpack_kernel,
        out_shape=(out, out),
        in_specs=[vmem],
        out_specs=(vmem, vmem),
        name="outputs",
    )(both)


def solution(mesh):
    placed = (
        P("blk", "rep"),
        P("blk", "rep"),
        P("blk", "rep", None, None),
        P("blk", "rep", None, None),
        P(),
        P(),
        P("blk"),
    )
    return jax.shard_map(
        shards,
        mesh=mesh,
        in_specs=placed,
        out_specs=(P("blk", "rep", None, None), P("blk", "rep", None, None)),
        check_vma=False,
    )
```
